512 devices in a mesh: leaf: 512 (over x, y, z, core).
Axes of the slice: x: 4, y: 4, z: 16, core: 2. Of those that a mesh axis runs over, the one named last changes fastest.
Arguments:
- right_sides: float32 [16, 1048576], P(None, 'leaf'), may hold values from -6 to 6
- coordinates: bfloat16 [3, 1048576], P(None, 'leaf'), may hold values from 0 to 4
- tree_order: int32 [1048576], P('leaf'), may hold values from 0 to 2047, as said below
- leaf_basis: bfloat16 [8192, 64, 128], P('leaf'), may hold values from -0.5 to 0.5
- far_pairs: int32 [2, 65536], P(None, 'leaf'), may hold values from 0 to 15, as said below
- far_coupling: bfloat16 [65536, 64, 64], P('leaf'), may hold values from -0.25 to 0.25
- near_pairs: int32 [2, 24576], P(None, 'leaf'), may hold values from 0 to 17, as said below
- leaf_transfer: bfloat16 [8192, 64, 64], P('leaf'), may hold values from -0.25 to 0.25
- top_transfer: bfloat16 [9, 2, 64, 64], replicated, may hold values from -0.625 to 0.625
- top_coupling: bfloat16 [9, 2, 64, 64], replicated, may hold values from -0.75 to 0.75
Outputs:
- product: float32 [16, 1048576], P(None, 'leaf')
The draws below stay inside these ranges and needn't reach their ends.
Inputs may be any that keep to these rules, and one draw needn't show every extreme that they name: `tree_order`: each subtree's block of 2048 entries is a permutation of 0 to 2047. `near_pairs`: in each subtree's block of 48 columns, row 0 names every local leaf exactly three times (values up to 15), once with itself as source (source = target + 1); row 1 values 0 and 17 each appear exactly once per block. `far_pairs`: in each subtree's block of 128 columns, every local leaf is target exactly 8 times with distinct sources, none of which is a near-field source of that target.
All inputs are finite; a program needn't handle non-finite values.
Results may differ from the reference program's by a relative error of at most 0.0031.
Values may be sent and summed in bfloat16 or wider, within the bound.
No kernel may reach another device: no remote copies, remote signals or barrier semaphores. Data moves between devices by JAX's collectives and lax.ppermute only.
A program may use at most 64 MiB of HBM per device.

```python
import jax
import jax.numpy as jnp
from jax import lax

LEAF = 128
R = 64
NRHS = 16
ADM = 8
LEAVES_DEV = 16
SUBTREES = 512
PTS_DEV = 2048
NODES = 8192
POINTS = 1048576
LEVELS = 9


def cycle_order(key):
    keys = jax.random.split(key, SUBTREES)
    return jax.vmap(lambda single: jax.random.permutation(single, LEAVES_DEV))(keys).astype(jnp.int32)


def draw_tree_order(key, part):
    key = jax.random.fold_in(key, 7)
    keys = jax.random.split(key, SUBTREES)
    orders = jax.vmap(lambda single: jax.random.permutation(single, PTS_DEV))(keys)
    return orders.reshape(-1).astype(jnp.int32)


def draw_near_pairs(key, part):
    cycle = cycle_order(key)
    positions = jnp.arange(LEAVES_DEV, dtype=jnp.int32)[None, :]
    before = jnp.where(positions == 0, 0, jnp.roll(cycle, 1, axis=1) + 1)
    after = jnp.where(positions == LEAVES_DEV - 1, LEAVES_DEV + 1, jnp.roll(cycle, -1, axis=1) + 1)
    sources = jnp.stack([before, cycle + 1, after], axis=2)
    targets = jnp.broadcast_to(cycle[:, :, None], sources.shape)
    return jnp.stack([targets.reshape(-1), sources.reshape(-1)], axis=0).astype(jnp.int32)


def draw_far_pairs(key, part):
    cycle = cycle_order(key)
    sources = jnp.stack([jnp.roll(cycle, -(2 + offset), axis=1) for offset in range(ADM)], axis=2)
    targets = jnp.broadcast_to(cycle[:, :, None], sources.shape)
    return jnp.stack([targets.reshape(-1), sources.reshape(-1)], axis=0).astype(jnp.int32)


def level_of(own_key, shape, cuts, least, top_value):
    def one(position, shards_of):
        draws = jax.random.uniform(jax.random.fold_in(jax.random.fold_in(own_key, 6), position), (shards_of,), jnp.float32, least / len(cuts), top_value / len(cuts))
        return jnp.repeat(jnp.exp(draws), shape[position] // shards_of).reshape((-1,) + (1,) * (len(shape) - position - 1))

    loudness = one(*cuts[0])
    for cut in cuts[1:]:
        loudness = loudness * one(*cut)
    return loudness


def scatter_about(rng, extent, scale, bound, pieces=(), kind=jnp.bfloat16):
    entries = scale * jax.random.normal(rng, extent, jnp.float32)
    if pieces:
        entries = entries * level_of(rng, extent, pieces, -0.22, 0.18)
    return jnp.clip(entries, -bound, bound).astype(kind)


def setup_inputs(seed: int = 0) -> dict:
    seeds = jax.random.split(jax.random.key(seed), 11)
    right_sides = scatter_about(seeds[0], (NRHS, POINTS), 1.0, 6.0, ((1, 512),), jnp.float32)
    coordinates = jnp.clip(4.0 * jax.random.uniform(seeds[1], (3, POINTS), jnp.float32) ** level_of(seeds[1], (3, POINTS), ((1, 512),), -0.2, 0.2), 0.0, 4.0).astype(jnp.bfloat16)
    tree_order = draw_tree_order(jax.random.fold_in(seeds[10], 71), 0)
    leaf_basis = scatter_about(seeds[3], (NODES, R, LEAF), LEAF ** -0.5, 0.5, ((0, 512),))
    far_pairs = draw_far_pairs(jax.random.fold_in(seeds[10], 71), 0)
    far_coupling = scatter_about(seeds[5], (NODES * ADM, R, R), (R * ADM) ** -0.5, 0.25, ((0, 512),))
    near_pairs = draw_near_pairs(jax.random.fold_in(seeds[10], 71), 0)
    leaf_transfer = scatter_about(seeds[7], (NODES, R, R), (R * LEAVES_DEV // 2) ** -0.5, 0.25, ((0, 512),))
    top_transfer = scatter_about(seeds[8], (LEVELS, 2, R, R), (R + R // 2) ** -0.5, 0.625)
    top_coupling = scatter_about(seeds[9], (LEVELS, 2, R, R), R ** -0.5, 0.75)
    return {"right_sides": right_sides, "coordinates": coordinates, "tree_order": tree_order, "leaf_basis": leaf_basis, "far_pairs": far_pairs, "far_coupling": far_coupling, "near_pairs": near_pairs, "leaf_transfer": leaf_transfer, "top_transfer": top_transfer, "top_coupling": top_coupling}


HIGH = lax.Precision.HIGHEST
SQRT_THREE = 3.0 ** 0.5
KERNEL_SCALE = 0.125

def matern_block(targets, sources):
    squared = jnp.zeros((targets.shape[1], targets.shape[2], sources.shape[2]), jnp.float32)
    for dimension in range(3):
        difference = targets[dimension][:, :, None] - sources[dimension][:, None, :]
        squared = squared + difference * difference
    scaled = SQRT_THREE * jnp.sqrt(squared)
    return (KERNEL_SCALE * (1.0 + scaled) * jnp.exp(-scaled)).astype(jnp.bfloat16)

def local_section(inputs):
    padded, basis, far_dev, coupling, near_dev, transfer = inputs
    rhs_leaves = padded[:NRHS, 1:-1].astype(jnp.float32)
    leaf_coef = jnp.einsum('trp,ktp->tkr', basis.astype(jnp.float32), rhs_leaves, precision=HIGH)
    targets = jnp.take(padded[NRHS:], near_dev[0] + 1, axis=1).astype(jnp.float32)
    sources = jnp.take(padded[NRHS:], near_dev[1], axis=1).astype(jnp.float32)
    source_rhs = jnp.take(padded[:NRHS], near_dev[1], axis=1).astype(jnp.float32)
    kernel = matern_block(targets, sources)
    contrib = jnp.einsum('nts,kns->nkt', kernel.astype(jnp.float32), source_rhs, precision=HIGH)
    near_sum = jax.ops.segment_sum(contrib, near_dev[0], LEAVES_DEV).transpose(1, 0, 2)
    gathered = leaf_coef[far_dev[1]]
    far_terms = jnp.einsum('nab,nkb->nka', coupling.astype(jnp.float32), gathered, precision=HIGH)
    far_sum = jax.ops.segment_sum(far_terms, far_dev[0], LEAVES_DEV)
    root = jnp.einsum('tcp,tkc->kp', transfer.astype(jnp.float32), leaf_coef, precision=HIGH)
    return (near_sum, far_sum, root)

def finish_section(inputs):
    near_sum, far_sum, root_field, basis, transfer, order = inputs
    leaf_field = far_sum + jnp.einsum('tcp,kp->tkc', transfer.astype(jnp.float32), root_field, precision=HIGH)
    values = near_sum + jnp.einsum('trp,tkr->ktp', basis.astype(jnp.float32), leaf_field, precision=HIGH)
    flattened = values.reshape(NRHS, PTS_DEV)
    return jnp.zeros((NRHS, PTS_DEV), jnp.float32).at[:, order].set(flattened)

def reference(right_sides, coordinates, tree_order, leaf_basis, far_pairs, far_coupling, near_pairs, leaf_transfer, top_transfer, top_coupling):
    order = tree_order.reshape(SUBTREES, PTS_DEV)
    rhs_blocks = right_sides.reshape(NRHS, SUBTREES, PTS_DEV)
    point_blocks = coordinates.reshape(3, SUBTREES, PTS_DEV)
    sorted_rhs = jnp.take_along_axis(rhs_blocks, order[None], axis=2).astype(jnp.bfloat16)
    sorted_pts = jnp.take_along_axis(point_blocks, order[None], axis=2)
    stacked = jnp.concatenate([sorted_rhs, sorted_pts], axis=0)
    leaves = stacked.reshape(NRHS + 3, SUBTREES, LEAVES_DEV, LEAF)
    zero_leaf = jnp.zeros((NRHS + 3, 1, 1, LEAF), jnp.bfloat16)
    before = jnp.concatenate([zero_leaf, leaves[:, :-1, -1:]], axis=1)
    after = jnp.concatenate([leaves[:, 1:, :1], zero_leaf], axis=1)
    padded = jnp.concatenate([before, leaves, after], axis=2).transpose(1, 0, 2, 3)
    basis = leaf_basis.reshape(SUBTREES, LEAVES_DEV, R, LEAF)
    far_dev = far_pairs.reshape(2, SUBTREES, LEAVES_DEV * ADM).transpose(1, 0, 2)
    coupling = far_coupling.reshape(SUBTREES, LEAVES_DEV * ADM, R, R)
    near_dev = near_pairs.reshape(2, SUBTREES, LEAVES_DEV * 3).transpose(1, 0, 2)
    transfer = leaf_transfer.reshape(SUBTREES, LEAVES_DEV, R, R)
    near_all, far_all, roots = lax.map(local_section, (padded, basis, far_dev, coupling, near_dev, transfer))
    coefficients = [roots]
    for height in range(LEVELS - 1):
        paired = coefficients[height].reshape(-1, 2, NRHS, R)
        left_part = jnp.einsum('cp,nkc->nkp', top_transfer[height, 0].astype(jnp.float32), paired[:, 0], precision=HIGH)
        right_part = jnp.einsum('cp,nkc->nkp', top_transfer[height, 1].astype(jnp.float32), paired[:, 1], precision=HIGH)
        coefficients.append(left_part + right_part)
    field = jnp.zeros((1, NRHS, R), jnp.float32)
    for height in reversed(range(LEVELS)):
        paired = coefficients[height].reshape(-1, 2, NRHS, R)
        swapped = paired[:, ::-1]
        coupled = jnp.einsum('sab,nskb->nska', top_coupling[height].astype(jnp.float32), swapped, precision=HIGH)
        inherited = jnp.einsum('scp,nkp->nskc', top_transfer[height].astype(jnp.float32), field, precision=HIGH)
        field = (coupled + inherited).reshape(-1, NRHS, R)
    outputs = lax.map(finish_section, (near_all, far_all, field, basis, transfer, order))
    return outputs.transpose(1, 0, 2).reshape(NRHS, POINTS)
```

```python
import jax
import jax.numpy as jnp
from jax import lax
from jax.experimental import pallas as pl
from jax.experimental.pallas import tpu as pltpu
from jax.sharding import PartitionSpec as P

BF = jnp.bfloat16
F32 = jnp.float32
LEAF = 128
RANK = 64
COLS = 16
LEAVES = 16
PTS = LEAVES * LEAF
LOW = 5
HIGHS = 4
NLOW = 1 << LOW
NHIGH = 1 << HIGHS
VMEM = pl.BlockSpec(memory_space=pltpu.VMEM)
SMEM = pl.BlockSpec(memory_space=pltpu.SMEM)
ANY = pl.BlockSpec(memory_space=pl.ANY)


def halves(x):
    hi = x.astype(BF)
    return hi, (x - hi.astype(F32)).astype(BF)


def mm(a, b):
    return jnp.dot(a, b, preferred_element_type=F32)


def mm_nt(a, b):
    return lax.dot_general(a, b, (((1,), (1,)), ((), ())), preferred_element_type=F32)


def wide(a, b):
    ah, al = halves(a)
    bh, bl = halves(b)
    return mm(ah, bh) + (mm(ah, bl) + mm(al, bh))


def wide_nt(a, b):
    ah, al = halves(a)
    bh, bl = halves(b)
    return mm_nt(ah, bh) + (mm_nt(ah, bl) + mm_nt(al, bh))


def low_onehot(order):
    lane = jnp.bitwise_and(order, LEAF - 1)
    rows = lax.broadcasted_iota(jnp.int32, (LEAF, order.shape[1]), 0)
    return jnp.where(rows == lane, 1.0, 0.0).astype(BF)


def permuted(x, order, width):
    stacked = jnp.concatenate([x[:, h * LEAF : (h + 1) * LEAF] for h in range(LEAVES)], axis=0)
    rows = x.shape[0]
    for start in range(0, order.shape[1], width):
        piece = order[:, start : start + width]
        picked = mm(stacked, low_onehot(piece))
        block = jnp.right_shift(piece, 7)
        total = jnp.zeros((rows, width), F32)
        for h in range(LEAVES):
            total = total + jnp.where(block == h, picked[h * rows : (h + 1) * rows], 0.0)
        yield start, total.astype(BF)


def pack_message(x):
    return jnp.concatenate([x[:8], x[8:]], axis=1)


def up_kernel(rhs_ref, order_ref, basis_ref, transfer_ref, sorted_ref, coef_ref, message_ref):
    x = rhs_ref[...].astype(BF)
    order = order_ref[...]
    root = jnp.zeros((2 * COLS, RANK), F32)
    for start, piece in permuted(x, order, 2 * LEAF):
        sorted_ref[:, start : start + 2 * LEAF] = piece
        for i in range(2):
            n = start // LEAF + i
            coef = mm_nt(piece[:, i * LEAF : (i + 1) * LEAF], basis_ref[n])
            hi, lo = halves(coef)
            both = jnp.concatenate([hi, lo], axis=0)
            coef_ref[n] = both
            root = root + mm(both, transfer_ref[n])
    message = pack_message(root[:COLS] + root[COLS:]).astype(BF)
    message_ref[...] = jnp.broadcast_to(message[None], message_ref.shape)


def points_kernel(coords_ref, order_ref, sorted_ref, head_ref, tail_ref, points_ref):
    x = jnp.concatenate([coords_ref[...], jnp.zeros((13, PTS), BF)], axis=0)
    for start, piece in permuted(x, order_ref[...], 2 * LEAF):
        points_ref[:, start : start + 2 * LEAF] = piece
    head_ref[0:COLS] = sorted_ref[:, 0:LEAF]
    head_ref[COLS:] = points_ref[:, 0:LEAF]
    tail_ref[0:COLS] = sorted_ref[:, PTS - LEAF :]
    tail_ref[COLS:] = points_ref[:, PTS - LEAF :]


def far_kernel(pairs_ref, coef_ref, coupling_ref, basis_ref, out_ref, acc):
    acc[...] = jnp.zeros_like(acc)
    for j in range(LEAVES * 8):
        target, source = pairs_ref[0, j], pairs_ref[1, j]
        acc[target] += mm_nt(coef_ref[source], coupling_ref[j])
    for n in range(LEAVES):
        total = acc[n]
        hi, lo = halves(total[:COLS] + total[COLS:])
        both = mm(jnp.concatenate([hi, lo], axis=0), basis_ref[n])
        out_ref[:, n * LEAF : (n + 1) * LEAF] = both[:COLS] + both[COLS:]


def point_features(points):
    p = points.astype(F32)
    x, y, z = p[0:1], p[1:2], p[2:3]
    square = x * x + y * y + z * z
    s0 = square.astype(BF).astype(F32)
    rest = square - s0
    s1 = rest.astype(BF).astype(F32)
    s2 = rest - s1
    one = jnp.ones_like(square)
    zero = jnp.zeros((7, LEAF), F32)
    source = jnp.concatenate([x, y, z, one, one, one, s0, s1, s2, zero], axis=0)
    target = jnp.concatenate(
        [-2.0 * x, -2.0 * y, -2.0 * z, s0, s1, s2, one, one, one, zero], axis=0
    )
    return source, target


def near_kernel(
    pairs_ref, sorted_ref, points_ref, left_ref, right_ref, far_ref, after_ref, out_ref, rhs, source, target, acc
):
    del after_ref
    for n in range(LEAVES + 2):
        if n == 0:
            columns, points = left_ref[0:COLS], left_ref[COLS:]
        elif n == LEAVES + 1:
            columns, points = right_ref[0:COLS], right_ref[COLS:]
        else:
            here = slice((n - 1) * LEAF, n * LEAF)
            columns, points = sorted_ref[:, here], points_ref[:, here]
        rhs[n] = columns
        of_source, of_target = point_features(points)
        source[n] = of_source.T.astype(BF)
        target[n] = of_target.astype(BF)
    for n in range(LEAVES):
        acc[n] = far_ref[:, n * LEAF : (n + 1) * LEAF]

    for j in range(LEAVES * 3):
        to, of = pairs_ref[0, j], pairs_ref[1, j]
        squared = jnp.maximum(mm(source[of], target[to + 1]), 0.0)
        scaled = jnp.sqrt(3.0 * squared)
        values = ((0.125 + 0.125 * scaled) * jnp.exp(-scaled)).astype(BF)
        acc[to] += mm(rhs[of], values)
    for n in range(LEAVES):
        out_ref[:, n * LEAF : (n + 1) * LEAF] = acc[n]


def chains(transfer_ref, first, count, tree):
    for h in range(count):
        size = 1 << h
        for side in range(2):
            step = transfer_ref[first + h, side].astype(F32)
            if h == 0:
                tree[0][side] = step
            else:
                rows = tree[h - 1][...].reshape(size * RANK, RANK)
                hi, lo = halves(rows)
                step = step.astype(BF)
                tree[h][side * size : (side + 1) * size] = (mm(hi, step) + mm(lo, step)).reshape(
                    size, RANK, RANK
                )


def weights_kernel(device_ref, transfer_ref, coupling_ref, low_ref, high_ref, *tree):
    device = device_ref[0]
    low_tree, high_tree = tree[:LOW], tree[LOW:]
    chains(transfer_ref, 0, LOW, low_tree)
    chains(transfer_ref, LOW, HIGHS, high_tree)

    def own(index, count, branch):
        return branch[count - 1][jnp.bitwise_and(index, (1 << count) - 1)]

    def store(ref, at, count, lane, value):
        hi, lo = halves(value)
        ref[pl.ds(at, count), :, lane : lane + RANK] = hi.reshape(count, RANK, RANK)
        ref[pl.ds(at, count), :, lane + 2 * RANK : lane + 3 * RANK] = lo.reshape(count, RANK, RANK)

    low = jnp.bitwise_and(device, NLOW - 1)
    store(low_ref, 0, NLOW, 0, low_tree[LOW - 1][...].reshape(NLOW * RANK, RANK))
    store(low_ref, low, 1, RANK, jnp.zeros((RANK, RANK), F32))
    for h in range(LOW):
        node = jnp.right_shift(low, h)
        coupling = coupling_ref[h, jnp.bitwise_and(node, 1)]
        at = jnp.left_shift(jnp.bitwise_xor(node, 1), h)
        if h == 0:
            value = coupling.astype(F32).T
        else:
            hi, lo = halves(own(low, h, low_tree))
            end = mm(hi, coupling) + mm(lo, coupling)
            value = wide_nt(low_tree[h - 1][...].reshape(-1, RANK), end)
        store(low_ref, at, 1 << h, RANK, value)

    high = jnp.right_shift(device, LOW)
    high_ref[pl.ds(high, 1)] = jnp.zeros((1, RANK, 2 * RANK), BF)
    bottom = own(low, LOW, low_tree)
    for h in range(HIGHS):
        node = jnp.right_shift(high, h)
        coupling = coupling_ref[LOW + h, jnp.bitwise_and(node, 1)]
        at = jnp.left_shift(jnp.bitwise_xor(node, 1), h)
        path = bottom if h == 0 else wide(bottom, own(high, h, high_tree))
        hi, lo = halves(path)
        end = mm(hi, coupling) + mm(lo, coupling)
        value = end.T if h == 0 else wide_nt(high_tree[h - 1][...].reshape(-1, RANK), end)
        hi, lo = halves(value)
        high_ref[pl.ds(at, 1 << h), :, 0:RANK] = hi.reshape(-1, RANK, RANK)
        high_ref[pl.ds(at, 1 << h), :, RANK : 2 * RANK] = lo.reshape(-1, RANK, RANK)


def unpacked(message):
    return jnp.concatenate([message[:, :RANK], message[:, RANK:]], axis=0)


def middle_kernel(received_ref, weight_ref, message_ref, field_ref):
    total = jnp.zeros((COLS, 4 * RANK), F32)
    for s in range(NLOW):
        total = total + mm(unpacked(received_ref[s]), weight_ref[s])
    total = total[:, : 2 * RANK] + total[:, 2 * RANK :]
    field_ref[...] = total[:, RANK:]
    message_ref[...] = jnp.broadcast_to(pack_message(total[:, :RANK])[None], message_ref.shape)


def down_kernel(
    received_ref, weight_ref, field_ref, partial_ref, transfer_ref, basis_ref, order_ref, out_ref
):
    total = jnp.zeros((2 * COLS, 2 * RANK), F32)
    for g in range(NHIGH):
        hi, lo = halves(unpacked(received_ref[g]))
        total = total + mm(jnp.concatenate([hi, lo], axis=0), weight_ref[g])
    total = total[:COLS] + total[COLS:]
    field = field_ref[...] + (total[:, :RANK] + total[:, RANK:])
    hi, lo = halves(field)
    field = jnp.concatenate([hi, lo], axis=0)
    result = [jnp.zeros((COLS, LEAF), F32) for _ in range(LEAVES)]
    result = jnp.zeros((LEAVES * 2 * COLS, LEAF), F32)
    order = order_ref[...]
    for start in range(0, PTS, 2 * LEAF):
        pieces = []
        for n in range(start // LEAF, start // LEAF + 2):
            leaf_field = mm_nt(field, transfer_ref[n])
            hi, lo = halves(leaf_field[:COLS] + leaf_field[COLS:])
            both = mm(jnp.concatenate([hi, lo], axis=0), basis_ref[n])
            pieces.append(both[:COLS] + both[COLS:])
        values = jnp.concatenate(pieces, axis=1) + partial_ref[:, start : start + 2 * LEAF]
        hi, lo = halves(values)
        both = jnp.concatenate([hi, lo], axis=0)
        piece = order[:, start : start + 2 * LEAF]
        block = jnp.right_shift(piece, 7)
        masked = jnp.concatenate(
            [both * jnp.where(block == h, 1.0, 0.0).astype(BF) for h in range(LEAVES)], axis=0
        )
        result = result + mm_nt(masked, low_onehot(piece))
    for h in range(LEAVES):
        at = h * 2 * COLS
        out_ref[:, h * LEAF : (h + 1) * LEAF] = result[at : at + COLS] + result[at + COLS : at + 2 * COLS]


def call(kernel, out, specs, args, scratch=(), flops=0, transcendentals=0, moved=1 << 20):
    shapes = [jax.ShapeDtypeStruct(s, t) for s, t in out]
    result = pl.pallas_call(
        kernel,
        out_shape=shapes,
        in_specs=specs,
        out_specs=[VMEM] * len(out),
        scratch_shapes=list(scratch),
        compiler_params=pltpu.CompilerParams(vmem_limit_bytes=40 << 20),
        cost_estimate=pl.CostEstimate(
            flops=flops, bytes_accessed=moved, transcendentals=transcendentals
        ),
    )(*args)
    return result


def per_device(
    right_sides,
    coordinates,
    tree_order,
    leaf_basis,
    far_pairs,
    far_coupling,
    near_pairs,
    leaf_transfer,
    top_transfer,
    top_coupling,
):
    count = lax.axis_size("leaf")
    device = lax.axis_index("leaf").astype(jnp.int32).reshape(1)
    order = tree_order.reshape(1, PTS)
    sorted_rhs, coef, message = call(
        up_kernel,
        [((COLS, PTS), BF), ((LEAVES, 2 * COLS, RANK), BF), ((NLOW, 8, 2 * RANK), BF)],
        [VMEM] * 4,
        (right_sides, order, leaf_basis, leaf_transfer),
        flops=1 << 28,
    )
    low_groups = [[g * NLOW + s for s in range(NLOW)] for g in range(NHIGH)]
    high_groups = [[g * NLOW + s for g in range(NHIGH)] for s in range(NLOW)]
    received = lax.all_to_all(message, "leaf", 0, 0, axis_index_groups=low_groups, tiled=True)

    head, tail, points = call(
        points_kernel,
        [((2 * COLS, LEAF), BF), ((2 * COLS, LEAF), BF), ((COLS, PTS), BF)],
        [VMEM] * 3,
        (coordinates, order, sorted_rhs),
        flops=1 << 30,
    )
    left = lax.ppermute(tail, "leaf", [(i, i + 1) for i in range(count - 1)])
    right = lax.ppermute(head, "leaf", [(i + 1, i) for i in range(count - 1)])
    low_weight, high_weight = call(
        weights_kernel,
        [((NLOW, RANK, 4 * RANK), BF), ((NHIGH, RANK, 2 * RANK), BF)],
        [SMEM, VMEM, VMEM],
        (device, top_transfer, top_coupling),
        scratch=[pltpu.VMEM((2 << h, RANK, RANK), F32) for h in range(LOW)]
        + [pltpu.VMEM((2 << h, RANK, RANK), F32) for h in range(HIGHS)],
        flops=1 << 31,
    )
    (far,) = call(
        far_kernel,
        [((COLS, PTS), F32)],
        [SMEM, VMEM, VMEM, VMEM],
        (far_pairs, coef, far_coupling, leaf_basis),
        scratch=[pltpu.VMEM((LEAVES, 2 * COLS, RANK), F32)],
        flops=1 << 31,
    )
    message, field = call(
        middle_kernel,
        [((NHIGH, 8, 2 * RANK), F32), ((COLS, RANK), F32)],
        [VMEM] * 2,
        (received, low_weight),
        flops=1 << 27,
    )
    received = lax.all_to_all(message, "leaf", 0, 0, axis_index_groups=high_groups, tiled=True)
    (partial,) = call(
        near_kernel,
        [((COLS, PTS), F32)],
        [SMEM] + [VMEM] * 5 + [ANY],
        (near_pairs, sorted_rhs, points, left, right, far, field),
        scratch=[
            pltpu.VMEM((LEAVES + 2, COLS, LEAF), BF),
            pltpu.VMEM((LEAVES + 2, LEAF, COLS), BF),
            pltpu.VMEM((LEAVES + 2, COLS, LEAF), BF),
            pltpu.VMEM((LEAVES, COLS, LEAF), F32),
        ],
        flops=1 << 32,
        transcendentals=1 << 21,
    )
    (product,) = call(
        down_kernel,
        [((COLS, PTS), F32)],
        [VMEM] * 7,
        (received, high_weight, field, partial, leaf_transfer, leaf_basis, order),
        flops=1 << 28,
    )
    return product


def solution(mesh):
    return jax.shard_map(
        per_device,
        mesh=mesh,
        in_specs=(
            P(None, "leaf"),
            P(None, "leaf"),
            P("leaf"),
            P("leaf", None, None),
            P(None, "leaf"),
            P("leaf", None, None),
            P(None, "leaf"),
            P("leaf", None, None),
            P(),
            P(),
        ),
        out_specs=P(None, "leaf"),
        check_vma=False,
    )
```

```python
import jax
import jax.numpy as jnp
from jax import lax
from jax.experimental import pallas as pl
from jax.experimental.pallas import tpu as pltpu
from jax.sharding import PartitionSpec as P

BF = jnp.bfloat16
F32 = jnp.float32
LEAF = 128
RANK = 64
COLS = 16
LEAVES = 16
PTS = LEAVES * LEAF
LOW = 4
HIGHS = 4
NLOW = 1 << LOW
NHIGH = 1 << HIGHS
VMEM = pl.BlockSpec(memory_space=pltpu.VMEM)
SMEM = pl.BlockSpec(memory_space=pltpu.SMEM)
ANY = pl.BlockSpec(memory_space=pl.ANY)
HBM = pl.BlockSpec(memory_space=pltpu.HBM)


def halves(x):
    hi = x.astype(BF)
    return hi, (x - hi.astype(F32)).astype(BF)


def mm(a, b):
    return jnp.dot(a, b, preferred_element_type=F32)


def mm_nt(a, b):
    return lax.dot_general(a, b, (((1,), (1,)), ((), ())), preferred_element_type=F32)


def wide(a, b):
    ah, al = halves(a)
    bh, bl = halves(b)
    return mm(ah, bh) + (mm(ah, bl) + mm(al, bh))


def wide_nt(a, b):
    ah, al = halves(a)
    bh, bl = halves(b)
    return mm_nt(ah, bh) + (mm_nt(ah, bl) + mm_nt(al, bh))


def low_onehot(order):
    lane = jnp.bitwise_and(order, LEAF - 1)
    rows = lax.broadcasted_iota(jnp.int32, (LEAF, order.shape[1]), 0)
    return jnp.where(rows == lane, 1.0, 0.0).astype(BF)


def permuted(x, order, width):
    stacked = jnp.concatenate([x[:, h * LEAF : (h + 1) * LEAF] for h in range(LEAVES)], axis=0)
    rows = x.shape[0]
    for start in range(0, order.shape[1], width):
        piece = order[:, start : start + width]
        picked = mm(stacked, low_onehot(piece))
        block = jnp.right_shift(piece, 7)
        total = jnp.zeros((rows, width), F32)
        for h in range(LEAVES):
            total = total + jnp.where(block == h, picked[h * rows : (h + 1) * rows], 0.0)
        yield start, total.astype(BF)


def pack_message(x):
    return jnp.concatenate([x[:8], x[8:]], axis=1)


def fetch(sources, buffers, sems):
    copies = [
        pltpu.make_async_copy(source, buffer, sems.at[i])
        for i, (source, buffer) in enumerate(zip(sources, buffers, strict=True))
    ]
    for copy in copies:
        copy.start()
    return copies


def up_kernel(
    order_hbm, rhs_hbm, basis_hbm, transfer_hbm, sorted_ref, coef_ref, message_ref, order_ref, rhs_ref, basis_ref, transfer_ref, sems
):
    copies = fetch(
        (order_hbm, rhs_hbm, basis_hbm, transfer_hbm),
        (order_ref, rhs_ref, basis_ref, transfer_ref),
        sems,
    )
    copies[0].wait()
    copies[1].wait()
    x = rhs_ref[...].astype(BF)
    order = order_ref[...]
    root = jnp.zeros((2 * COLS, RANK), F32)
    for start, piece in permuted(x, order, 2 * LEAF):
        sorted_ref[:, start : start + 2 * LEAF] = piece
        if start == 0:
            copies[2].wait()
            copies[3].wait()
        for i in range(2):
            n = start // LEAF + i
            coef = mm_nt(piece[:, i * LEAF : (i + 1) * LEAF], basis_ref[n])
            hi, lo = halves(coef)
            both = jnp.concatenate([hi, lo], axis=0)
            coef_ref[n] = coef
            root = root + mm(both, transfer_ref[n])
    message = pack_message(root[:COLS] + root[COLS:])
    message_ref[...] = jnp.broadcast_to(message[None], message_ref.shape)


def points_kernel(device_ref, coords_hbm, order_hbm, sorted_ref, near_ref, across_ref, points_ref, coords_ref, order_ref, sems):
    copies = fetch((coords_hbm, order_hbm), (coords_ref, order_ref), sems)
    for copy in copies:
        copy.wait()
    x = jnp.concatenate([coords_ref[...], jnp.zeros((13, PTS), BF)], axis=0)
    for start, piece in permuted(x, order_ref[...], 2 * LEAF):
        points_ref[:, start : start + 2 * LEAF] = piece
    head = jnp.concatenate([sorted_ref[:, 0:LEAF], points_ref[:, 0:LEAF]], axis=0)
    tail = jnp.concatenate([sorted_ref[:, PTS - LEAF :], points_ref[:, PTS - LEAF :]], axis=0)
    even = jnp.bitwise_and(device_ref[0], 1) == 0

    @pl.when(even)
    def _():
        near_ref[...] = tail
        across_ref[...] = head

    @pl.when(jnp.logical_not(even))
    def _():
        near_ref[...] = head
        across_ref[...] = tail


def far_kernel(
    after_ref, coef_ref, pairs_hbm, coupling_hbm, basis_hbm, out_ref, pairs_ref, coupling_ref, basis_ref, by_column, picked, terms, fields, sems
):
    del after_ref
    copies = fetch(
        (pairs_hbm, coupling_hbm, basis_hbm), (pairs_ref, coupling_ref, basis_ref), sems
    )
    for n in range(LEAVES):
        by_column[:, n, :] = coef_ref[n]
    copies[0].wait()
    rows = lax.broadcasted_iota(jnp.int32, (LEAVES, LEAF), 0)
    targets = jnp.where(rows == pairs_ref[0:1, :], 1.0, 0.0).astype(BF)
    sources = jnp.where(rows == pairs_ref[1:2, :], 1.0, 0.0).astype(BF)
    sources = jnp.concatenate([sources, sources], axis=0)
    for k in range(COLS):
        hi, lo = halves(by_column[k])
        both = jnp.concatenate([hi, lo], axis=0)
        picked[k] = lax.dot_general(
            both, sources, (((0,), (0,)), ((), ())), preferred_element_type=F32
        )
    copies[1].wait()
    step = 8

    def some_rows(i, carry):
        at = pl.multiple_of(i * step, step)
        block = coupling_ref[pl.ds(at, step)].astype(F32)
        for k in range(COLS):
            terms[k, pl.ds(at, step), :] = jnp.sum(block * picked[k][None], axis=1)
        return carry

    lax.fori_loop(0, RANK // step, some_rows, 0)
    for k in range(COLS):
        hi, lo = halves(terms[k])
        fields[:, k, :] = mm_nt(targets, hi) + mm_nt(targets, lo)
    copies[2].wait()
    for n in range(LEAVES):
        hi, lo = halves(fields[n])
        both = mm(jnp.concatenate([hi, lo], axis=0), basis_ref[n])
        out_ref[:, n * LEAF : (n + 1) * LEAF] = both[:COLS] + both[COLS:]


def point_features(points):
    p = points.astype(F32)
    x, y, z = p[0:1], p[1:2], p[2:3]
    square = x * x + y * y + z * z
    s0 = square.astype(BF).astype(F32)
    rest = square - s0
    s1 = rest.astype(BF).astype(F32)
    s2 = rest - s1
    one = jnp.ones_like(square)
    zero = jnp.zeros((7, LEAF), F32)
    source = jnp.concatenate([x, y, z, one, one, one, s0, s1, s2, zero], axis=0)
    target = jnp.concatenate(
        [-2.0 * x, -2.0 * y, -2.0 * z, s0, s1, s2, one, one, one, zero], axis=0
    )
    return source, target


def near_kernel(
    device_ref, pairs_ref, sorted_ref, points_ref, inner_ref, across_ref, far_ref, out_ref, rhs, source, target, acc
):
    even = jnp.bitwise_and(device_ref[0], 1) == 0
    inner, across = inner_ref[...], across_ref[...]

    def prepare(n, columns, points):
        rhs[n] = columns
        of_source, of_target = point_features(points)
        source[n] = of_source.T.astype(BF)
        target[n] = of_target.astype(BF)

    prepare(jnp.where(even, LEAVES + 1, 0), inner[:COLS], inner[COLS:])
    prepare(jnp.where(even, 0, LEAVES + 1), across[:COLS], across[COLS:])
    for n in range(LEAVES):
        here = slice(n * LEAF, (n + 1) * LEAF)
        prepare(n + 1, sorted_ref[:, here], points_ref[:, here])
        acc[n] = far_ref[:, here]

    for j in range(LEAVES * 3):
        to, of = pairs_ref[0, j], pairs_ref[1, j]
        squared = jnp.maximum(mm(source[of], target[to + 1]), 0.0)
        scaled = jnp.sqrt(3.0 * squared)
        values = ((0.125 + 0.125 * scaled) * jnp.exp(-scaled)).astype(BF)
        acc[to] += mm(rhs[of], values)
    for n in range(LEAVES):
        out_ref[:, n * LEAF : (n + 1) * LEAF] = acc[n]


def times(a, b):
    hi, lo = halves(a)
    both = mm(jnp.concatenate([hi, lo], axis=0), b)
    return both[: a.shape[0]] + both[a.shape[0] :]


def weights_kernel(device_ref, transfer_hbm, coupling_hbm, low_ref, high_ref, transfer_ref, coupling_ref, sems):
    copies = fetch((transfer_hbm, coupling_hbm), (transfer_ref, coupling_ref), sems)
    device = device_ref[0]
    core = jnp.bitwise_and(device, 1)
    low = jnp.bitwise_and(jnp.right_shift(device, 1), NLOW - 1)
    high = jnp.right_shift(device, LOW + 1)
    for copy in copies:
        copy.wait()
    mine, other = transfer_ref[0, core], transfer_ref[0, 1 - core]

    hi, lo = halves(coupling_ref[0, 1 - core].astype(F32).T)
    zero = jnp.zeros((RANK, RANK), BF)
    low_ref[pl.ds(low, 1), :, 2 * RANK :] = jnp.concatenate([zero, hi, zero, lo], axis=1)[None]

    senders = mine.astype(F32)
    path = jnp.concatenate([mine, other], axis=0).astype(F32)
    for level in range(1, LOW + 1):
        h = level - 1
        node = jnp.right_shift(low, h)
        side = jnp.bitwise_and(node, 1)
        at = jnp.left_shift(jnp.bitwise_xor(node, 1), h)
        end = times(path, coupling_ref[level, side])
        hi, lo = halves(wide_nt(senders, end))
        low_ref[pl.ds(at, 1 << h), :, 2 * RANK :] = jnp.concatenate([hi, lo], axis=1).reshape(
            1 << h, RANK, 4 * RANK
        )
        path = times(path, transfer_ref[level, side])
        senders = jnp.concatenate(
            [times(senders, transfer_ref[level, 0]), times(senders, transfer_ref[level, 1])], axis=0
        )
    hi, lo = halves(senders)
    low_ref[:, :, : 2 * RANK] = jnp.concatenate([hi, lo], axis=1).reshape(NLOW, RANK, 2 * RANK)

    path = path[:RANK]
    high_ref[pl.ds(high, 1)] = jnp.zeros((1, RANK, 2 * RANK), BF)
    for h in range(HIGHS):
        level = LOW + 1 + h
        node = jnp.right_shift(high, h)
        side = jnp.bitwise_and(node, 1)
        at = jnp.left_shift(jnp.bitwise_xor(node, 1), h)
        end = times(path, coupling_ref[level, side])
        hi, lo = halves(end.T if h == 0 else wide_nt(senders, end))
        high_ref[pl.ds(at, 1 << h)] = jnp.concatenate([hi, lo], axis=1).reshape(
            1 << h, RANK, 2 * RANK
        )
        if h == HIGHS - 1:
            break
        path = times(path, transfer_ref[level, side])
        if h == 0:
            senders = transfer_ref[level].reshape(2 * RANK, RANK).astype(F32)
        else:
            senders = jnp.concatenate(
                [times(senders, transfer_ref[level, 0]), times(senders, transfer_ref[level, 1])], axis=0
            )


def unpacked(message):
    x = jnp.concatenate([message[:, :RANK], message[:, RANK:]], axis=0)
    hi, lo = halves(x)
    return jnp.concatenate([hi, lo], axis=0)


def middle_kernel(device_ref, received_ref, weight_ref, message_ref, field_ref):
    device = device_ref[0]
    total = jnp.zeros((2 * COLS, 6 * RANK), F32)
    for s in range(NLOW):
        total = total + mm(unpacked(received_ref[s]), weight_ref[s])
    total = total[:COLS] + total[COLS:]
    node = total[:, :RANK] + total[:, RANK : 2 * RANK]
    fields = total[:, 2 * RANK : 4 * RANK] + total[:, 4 * RANK :]
    field_ref[...] = fields[:, :RANK]
    message_ref[...] = jnp.broadcast_to(pack_message(node)[None], message_ref.shape)
    high, core = jnp.right_shift(device, LOW + 1), jnp.bitwise_and(device, 1)
    message_ref[high * 2 + 1 - core] = pack_message(fields[:, RANK:])


def down_kernel(
    device_ref, received_ref, weight_ref, field_ref, partial_ref, transfer_hbm, basis_hbm, order_hbm, out_ref, transfer_ref, basis_ref, order_ref, sems
):
    copies = fetch(
        (transfer_hbm, basis_hbm, order_hbm), (transfer_ref, basis_ref, order_ref), sems
    )
    device = device_ref[0]
    high, core = jnp.right_shift(device, LOW + 1), jnp.bitwise_and(device, 1)
    total = jnp.zeros((2 * COLS, 2 * RANK), F32)
    for g in range(NHIGH):
        total = total + mm(unpacked(received_ref[2 * g] + received_ref[2 * g + 1]), weight_ref[g])
    total = total[:COLS] + total[COLS:]
    sibling = received_ref[high * 2 + 1 - core]
    field = field_ref[...] + (total[:, :RANK] + total[:, RANK:])
    field = field + jnp.concatenate([sibling[:, :RANK], sibling[:, RANK:]], axis=0)
    hi, lo = halves(field)
    field = jnp.concatenate([hi, lo], axis=0)
    result = jnp.zeros((LEAVES * 2 * COLS, LEAF), F32)
    for copy in copies:
        copy.wait()
    order = order_ref[...]
    for start in range(0, PTS, 2 * LEAF):
        pieces = []
        for n in range(start // LEAF, start // LEAF + 2):
            leaf_field = mm_nt(field, transfer_ref[n])
            hi, lo = halves(leaf_field[:COLS] + leaf_field[COLS:])
            both = mm(jnp.concatenate([hi, lo], axis=0), basis_ref[n])
            pieces.append(both[:COLS] + both[COLS:])
        values = jnp.concatenate(pieces, axis=1) + partial_ref[:, start : start + 2 * LEAF]
        hi, lo = halves(values)
        both = jnp.concatenate([hi, lo], axis=0)
        piece = order[:, start : start + 2 * LEAF]
        block = jnp.right_shift(piece, 7)
        masked = jnp.concatenate(
            [both * jnp.where(block == h, 1.0, 0.0).astype(BF) for h in range(LEAVES)], axis=0
        )
        result = result + mm_nt(masked, low_onehot(piece))
    for h in range(LEAVES):
        at = h * 2 * COLS
        out_ref[:, h * LEAF : (h + 1) * LEAF] = result[at : at + COLS] + result[at + COLS : at + 2 * COLS]


def call(kernel, out, inputs, buffers=(), scratch=(), flops=0, transcendentals=0):
    shapes = [jax.ShapeDtypeStruct(s, t) for s, t in out]
    scratches = [pltpu.VMEM(s, t) for s, t in buffers] + [pltpu.VMEM(s, t) for s, t in scratch]
    if buffers:
        scratches.append(pltpu.SemaphoreType.DMA((len(buffers),)))
    return pl.pallas_call(
        kernel,
        out_shape=shapes,
        in_specs=[space for space, _ in inputs],
        out_specs=[VMEM] * len(out),
        scratch_shapes=scratches,
        compiler_params=pltpu.CompilerParams(vmem_limit_bytes=16 << 20),
        cost_estimate=pl.CostEstimate(
            flops=flops, bytes_accessed=1 << 20, transcendentals=transcendentals
        ),
    )(*[array for _, array in inputs])


def per_device(
    right_sides,
    coordinates,
    tree_order,
    leaf_basis,
    far_pairs,
    far_coupling,
    near_pairs,
    leaf_transfer,
    top_transfer,
    top_coupling,
):
    count = lax.axis_size("leaf")
    device = lax.axis_index("leaf").astype(jnp.int32).reshape(1)
    order = tree_order.reshape(1, PTS)
    basis_like = (leaf_basis.shape, BF)
    transfer_like = (leaf_transfer.shape, BF)
    order_like = (order.shape, jnp.int32)
    sorted_rhs, coef, message = call(
        up_kernel,
        [((COLS, PTS), BF), ((LEAVES, COLS, RANK), F32), ((NLOW, 8, 2 * RANK), F32)],
        [(HBM, order), (HBM, right_sides), (HBM, leaf_basis), (HBM, leaf_transfer)],
        buffers=[order_like, (right_sides.shape, F32), basis_like, transfer_like],
        flops=1 << 28,
    )
    low_groups = [
        [(g * NLOW + z) * 2 + c for z in range(NLOW)] for g in range(NHIGH) for c in range(2)
    ]
    high_groups = [
        [(g * NLOW + z) * 2 + c for g in range(NHIGH) for c in range(2)] for z in range(NLOW)
    ]
    received = lax.all_to_all(message, "leaf", 0, 0, axis_index_groups=low_groups, tiled=True)

    inner, across, points = call(
        points_kernel,
        [((2 * COLS, LEAF), BF), ((2 * COLS, LEAF), BF), ((COLS, PTS), BF)],
        [(SMEM, device), (HBM, coordinates), (HBM, order), (VMEM, sorted_rhs)],
        buffers=[(coordinates.shape, BF), order_like],
        flops=1 << 28,
    )
    inner = lax.ppermute(inner, "leaf", [(i, i ^ 1) for i in range(count)])
    pairs = [(i, i + 1) for i in range(1, count - 1, 2)]
    across = lax.ppermute(across, "leaf", pairs + [(j, i) for i, j in pairs])
    low_weight, high_weight = call(
        weights_kernel,
        [((NLOW, RANK, 6 * RANK), BF), ((NHIGH, RANK, 2 * RANK), BF)],
        [(SMEM, device), (HBM, top_transfer), (HBM, top_coupling)],
        buffers=[(top_transfer.shape, BF), (top_coupling.shape, BF)],
        flops=1 << 30,
    )
    message, field = call(
        middle_kernel,
        [((2 * NHIGH, 8, 2 * RANK), F32), ((COLS, RANK), F32)],
        [(SMEM, device), (VMEM, received), (VMEM, low_weight)],
        flops=1 << 27,
    )
    received = lax.all_to_all(message, "leaf", 0, 0, axis_index_groups=high_groups, tiled=True)
    coupling = far_coupling.transpose(1, 2, 0)
    (far,) = call(
        far_kernel,
        [((COLS, PTS), F32)],
        [(ANY, field), (VMEM, coef), (HBM, far_pairs), (HBM, coupling), (HBM, leaf_basis)],
        buffers=[(far_pairs.shape, jnp.int32), (coupling.shape, BF), basis_like],
        scratch=[
            ((COLS, LEAVES, RANK), F32),
            ((COLS, RANK, LEAF), F32),
            ((COLS, RANK, LEAF), F32),
            ((LEAVES, COLS, RANK), F32),
        ],
        flops=1 << 31,
    )
    (partial,) = call(
        near_kernel,
        [((COLS, PTS), F32)],
        [
            (SMEM, device),
            (SMEM, near_pairs),
            (VMEM, sorted_rhs),
            (VMEM, points),
            (VMEM, inner),
            (VMEM, across),
            (VMEM, far),
        ],
        scratch=[
            ((LEAVES + 2, COLS, LEAF), BF),
            ((LEAVES + 2, LEAF, COLS), BF),
            ((LEAVES + 2, COLS, LEAF), BF),
            ((LEAVES, COLS, LEAF), F32),
        ],
        flops=1 << 31,
        transcendentals=1 << 21,
    )
    (product,) = call(
        down_kernel,
        [((COLS, PTS), F32)],
        [
            (SMEM, device),
            (VMEM, received),
            (VMEM, high_weight),
            (VMEM, field),
            (VMEM, partial),
            (HBM, leaf_transfer),
            (HBM, leaf_basis),
            (HBM, order),
        ],
        buffers=[transfer_like, basis_like, order_like],
        flops=1 << 28,
    )
    return product


def solution(mesh):
    return jax.shard_map(
        per_device,
        mesh=mesh,
        in_specs=(
            P(None, "leaf"),
            P(None, "leaf"),
            P("leaf"),
            P("leaf", None, None),
            P(None, "leaf"),
            P("leaf", None, None),
            P(None, "leaf"),
            P("leaf", None, None),
            P(),
            P(),
        ),
        out_specs=P(None, "leaf"),
        check_vma=False,
    )
```

```python
import jax
import jax.numpy as jnp
from jax import lax
from jax.experimental import pallas as pl
from jax.experimental.pallas import tpu as pltpu
from jax.sharding import PartitionSpec as P

BF = jnp.bfloat16
F32 = jnp.float32
LEAF = 128
RANK = 64
COLS = 16
LEAVES = 16
WIDE = 256
BLOCKS = 8
PTS = LEAVES * LEAF
LOW = 4
HIGHS = 4
NLOW = 1 << LOW
NHIGH = 1 << HIGHS
LOG2E = 1.4426950408889634
VMEM = pl.BlockSpec(memory_space=pltpu.VMEM)
SMEM = pl.BlockSpec(memory_space=pltpu.SMEM)
ANY = pl.BlockSpec(memory_space=pl.ANY)
HBM = pl.BlockSpec(memory_space=pltpu.HBM)


def halves(x):
    hi = x.astype(BF)
    return hi, (x - hi.astype(F32)).astype(BF)


def mm(a, b):
    return jnp.dot(a, b, preferred_element_type=F32)


def mm_nt(a, b):
    return lax.dot_general(a, b, (((1,), (1,)), ((), ())), preferred_element_type=F32)


def wide(a, b):
    ah, al = halves(a)
    bh, bl = halves(b)
    return mm(ah, bh) + (mm(ah, bl) + mm(al, bh))


def wide_nt(a, b):
    ah, al = halves(a)
    bh, bl = halves(b)
    return mm_nt(ah, bh) + (mm_nt(ah, bl) + mm_nt(al, bh))


def low_onehot(order):
    lane = jnp.bitwise_and(order, WIDE - 1).astype(F32).astype(BF)
    rows = lax.broadcasted_iota(jnp.int32, (WIDE, order.shape[1]), 0).astype(F32).astype(BF)
    return jnp.where(rows == lane, jnp.ones((), BF), jnp.zeros((), BF))


def permuted(x, order, width):
    stacked = jnp.concatenate([x[:, h * WIDE : (h + 1) * WIDE] for h in range(BLOCKS)], axis=0)
    rows = x.shape[0]
    for start in range(0, order.shape[1], width):
        piece = order[:, start : start + width]
        picked = mm(stacked, low_onehot(piece))
        block = jnp.right_shift(piece, 8)
        total = jnp.zeros((rows, width), F32)
        for h in range(BLOCKS):
            total = total + jnp.where(block == h, picked[h * rows : (h + 1) * rows], 0.0)
        yield start, total.astype(BF)


def pack_message(x):
    return jnp.concatenate([x[:8], x[8:]], axis=1)


def fetch(sources, buffers, sems):
    copies = [
        pltpu.make_async_copy(source, buffer, sems.at[i])
        for i, (source, buffer) in enumerate(zip(sources, buffers, strict=True))
    ]
    for copy in copies:
        copy.start()
    return copies


def up_kernel(
    order_hbm, rhs_hbm, basis_hbm, transfer_hbm, sorted_ref, coef_ref, message_ref, order_ref, rhs_ref, basis_ref, transfer_ref, sems
):
    copies = fetch(
        (order_hbm, rhs_hbm, basis_hbm, transfer_hbm),
        (order_ref, rhs_ref, basis_ref, transfer_ref),
        sems,
    )
    copies[0].wait()
    copies[1].wait()
    x = rhs_ref[...].astype(BF)
    order = order_ref[...]
    block = jnp.right_shift(order, 8)
    places = low_onehot(order)
    copies[2].wait()
    copies[3].wait()
    stacked = jnp.concatenate([x[:, h * WIDE : (h + 1) * WIDE] for h in range(BLOCKS)], axis=0)
    picked = mm(stacked, places)
    total = jnp.where(block == 0, picked[:COLS], 0.0)
    for h in range(1, BLOCKS):
        total = total + jnp.where(block == h, picked[h * COLS : (h + 1) * COLS], 0.0)
    total = total.astype(BF)
    sorted_ref[...] = total
    coefs = []
    for n in range(LEAVES):
        coef = mm_nt(total[:, n * LEAF : (n + 1) * LEAF], basis_ref[n])
        coefs.append(coef)
        coef_ref[n] = coef
    hi, lo = halves(jnp.concatenate(coefs, axis=1))
    root = mm(jnp.concatenate([hi, lo], axis=0), transfer_ref[...].reshape(LEAVES * RANK, RANK))
    message = pack_message(root[:COLS] + root[COLS:])
    message_ref[...] = jnp.broadcast_to(message[None], message_ref.shape)


def points_kernel(device_ref, coords_hbm, order_hbm, sorted_ref, near_ref, across_ref, points_ref, coords_ref, order_ref, sems):
    copies = fetch((coords_hbm, order_hbm), (coords_ref, order_ref), sems)
    for copy in copies:
        copy.wait()
    x = jnp.concatenate([coords_ref[...], jnp.zeros((13, PTS), BF)], axis=0)
    for start, piece in permuted(x, order_ref[...], 2 * LEAF):
        points_ref[:, start : start + 2 * LEAF] = piece
    head = jnp.concatenate([sorted_ref[:, 0:LEAF], points_ref[:, 0:LEAF]], axis=0)
    tail = jnp.concatenate([sorted_ref[:, PTS - LEAF :], points_ref[:, PTS - LEAF :]], axis=0)
    even = jnp.bitwise_and(device_ref[0], 1) == 0

    @pl.when(even)
    def _():
        near_ref[...] = tail
        across_ref[...] = head

    @pl.when(jnp.logical_not(even))
    def _():
        near_ref[...] = head
        across_ref[...] = tail


def point_features(points):
    p = points.astype(F32)
    x, y, z = p[0:1], p[1:2], p[2:3]
    square = x * x + y * y + z * z
    s0 = square.astype(BF).astype(F32)
    rest = square - s0
    s1 = rest.astype(BF).astype(F32)
    s2 = rest - s1
    one = jnp.ones_like(square)
    zero = jnp.zeros((7, points.shape[1]), F32)
    source = jnp.concatenate([x, y, z, one, one, one, s0, s1, s2, zero], axis=0)
    target = jnp.concatenate(
        [-2.0 * x, -2.0 * y, -2.0 * z, s0, s1, s2, one, one, one, zero], axis=0
    )
    return source, target


def local_kernel(
    device_ref, near_ref, far_ref, after_ref, coef_ref, coupling_ref, basis_ref, sorted_ref, points_ref, inner_ref, across_ref, out_ref,
    by_pair, spread, far, rhs, source, target, near
):
    del after_ref
    rows = lax.broadcasted_iota(jnp.int32, (LEAF, LEAF), 0)
    columns = lax.broadcasted_iota(jnp.int32, (LEAF, LEAF), 1)
    identity = jnp.where(rows == columns, 1.0, 0.0).astype(BF)
    for a in range(RANK // 2):
        two = jnp.concatenate([coupling_ref[a], coupling_ref[a + RANK // 2]], axis=0)
        by_pair[a * LEAF : (a + 1) * LEAF, :] = mm_nt(identity, two)
    zero = jnp.zeros((2 * COLS, RANK), BF)
    for n in range(LEAVES):
        hi, lo = halves(coef_ref[n])
        both = jnp.concatenate([hi, lo], axis=0)
        spread[n] = jnp.concatenate(
            [jnp.concatenate([both, zero], axis=1), jnp.concatenate([zero, both], axis=1)], axis=0
        )
    far[...] = jnp.zeros_like(far)
    near[...] = jnp.zeros_like(near)

    even = jnp.bitwise_and(device_ref[0], 1) == 0
    inner, across = inner_ref[...].astype(F32), across_ref[...].astype(F32)
    left = jnp.where(even, across, inner).astype(BF)
    right = jnp.where(even, inner, across).astype(BF)
    columns = jnp.concatenate([left[:COLS], sorted_ref[...], right[:COLS]], axis=1)
    points = jnp.concatenate([left[COLS:], points_ref[...], right[COLS:]], axis=1)
    of_source, of_target = point_features(points)
    of_target = of_target.astype(BF)
    for n in range(LEAVES + 2):
        here = slice(n * LEAF, (n + 1) * LEAF)
        rhs[n] = columns[:, here]
        source[n] = of_source[:, here].T.astype(BF)
        target[n] = of_target[:, here]

    def far_pair(j):
        to, of = far_ref[0, j], far_ref[1, j]
        rows = by_pair[pl.ds(j, RANK // 2, stride=LEAF), :].astype(BF)
        far[to] += mm_nt(rows, spread[of])

    def near_pair(j):
        to, of = near_ref[0, j], near_ref[1, j]
        squared = jnp.maximum(mm(source[of], target[to + 1]) * (3.0 * LOG2E * LOG2E), 1e-30)
        scaled = squared * lax.rsqrt(squared)
        values = ((0.125 + (0.125 / LOG2E) * scaled) * jnp.exp2(-scaled)).astype(BF)
        near[to] += mm(rhs[of], values)

    for j in range(8 * LEAVES):
        far_pair(j)
    for j in range(3 * LEAVES):
        near_pair(j)
    for n in range(LEAVES):
        x = far[n].T
        field = jnp.concatenate(
            [x[:COLS] + x[COLS : 2 * COLS], x[2 * COLS : 3 * COLS] + x[3 * COLS :]], axis=1
        )
        hi, lo = halves(field)
        both = mm(jnp.concatenate([hi, lo], axis=0), basis_ref[n])
        out_ref[:, n * LEAF : (n + 1) * LEAF] = near[n] + (both[:COLS] + both[COLS:])


def times(a, b):
    hi, lo = halves(a)
    both = mm(jnp.concatenate([hi, lo], axis=0), b)
    return both[: a.shape[0]] + both[a.shape[0] :]


def weights_kernel(device_ref, transfer_hbm, coupling_hbm, low_ref, high_ref, transfer_ref, coupling_ref, sems):
    copies = fetch((transfer_hbm, coupling_hbm), (transfer_ref, coupling_ref), sems)
    device = device_ref[0]
    core = jnp.bitwise_and(device, 1)
    low = jnp.bitwise_and(jnp.right_shift(device, 1), NLOW - 1)
    high = jnp.right_shift(device, LOW + 1)
    for copy in copies:
        copy.wait()
    mine, other = transfer_ref[0, core], transfer_ref[0, 1 - core]

    hi, lo = halves(coupling_ref[0, 1 - core].astype(F32).T)
    zero = jnp.zeros((RANK, RANK), BF)
    low_ref[pl.ds(low, 1), :, 2 * RANK :] = jnp.concatenate([zero, hi, zero, lo], axis=1)[None]

    senders = mine.astype(F32)
    path = jnp.concatenate([mine, other], axis=0).astype(F32)
    for level in range(1, LOW + 1):
        h = level - 1
        node = jnp.right_shift(low, h)
        side = jnp.bitwise_and(node, 1)
        at = jnp.left_shift(jnp.bitwise_xor(node, 1), h)
        end = times(path, coupling_ref[level, side])
        hi, lo = halves(wide_nt(senders, end))
        low_ref[pl.ds(at, 1 << h), :, 2 * RANK :] = jnp.concatenate([hi, lo], axis=1).reshape(
            1 << h, RANK, 4 * RANK
        )
        path = times(path, transfer_ref[level, side])
        senders = jnp.concatenate(
            [times(senders, transfer_ref[level, 0]), times(senders, transfer_ref[level, 1])], axis=0
        )
    hi, lo = halves(senders)
    low_ref[:, :, : 2 * RANK] = jnp.concatenate([hi, lo], axis=1).reshape(NLOW, RANK, 2 * RANK)

    path = path[:RANK]
    high_ref[pl.ds(high, 1)] = jnp.zeros((1, RANK, 2 * RANK), BF)
    for h in range(HIGHS):
        level = LOW + 1 + h
        node = jnp.right_shift(high, h)
        side = jnp.bitwise_and(node, 1)
        at = jnp.left_shift(jnp.bitwise_xor(node, 1), h)
        end = times(path, coupling_ref[level, side])
        hi, lo = halves(end.T if h == 0 else wide_nt(senders, end))
        high_ref[pl.ds(at, 1 << h)] = jnp.concatenate([hi, lo], axis=1).reshape(
            1 << h, RANK, 2 * RANK
        )
        if h == HIGHS - 1:
            break
        path = times(path, transfer_ref[level, side])
        if h == 0:
            senders = transfer_ref[level].reshape(2 * RANK, RANK).astype(F32)
        else:
            senders = jnp.concatenate(
                [times(senders, transfer_ref[level, 0]), times(senders, transfer_ref[level, 1])], axis=0
            )


def unpacked(messages):
    x = jnp.concatenate([m[:, :RANK] for m in messages], axis=1)
    y = jnp.concatenate([m[:, RANK:] for m in messages], axis=1)
    hi, lo = halves(jnp.concatenate([x, y], axis=0))
    return jnp.concatenate([hi, lo], axis=0)


def middle_kernel(device_ref, received_ref, weight_ref, message_ref, field_ref):
    device = device_ref[0]
    total = mm(
        unpacked([received_ref[s] for s in range(NLOW)]), weight_ref[...].reshape(NLOW * RANK, 6 * RANK)
    )
    total = total[:COLS] + total[COLS:]
    node = total[:, :RANK] + total[:, RANK : 2 * RANK]
    fields = total[:, 2 * RANK : 4 * RANK] + total[:, 4 * RANK :]
    field_ref[...] = fields[:, :RANK]
    message_ref[...] = jnp.broadcast_to(pack_message(node)[None], message_ref.shape)
    high, core = jnp.right_shift(device, LOW + 1), jnp.bitwise_and(device, 1)
    message_ref[high * 2 + 1 - core] = pack_message(fields[:, RANK:])


def down_kernel(
    device_ref, received_ref, weight_ref, field_ref, partial_ref, transfer_hbm, basis_hbm, order_hbm, out_ref, transfer_ref, basis_ref, order_ref, sems
):
    copies = fetch(
        (transfer_hbm, basis_hbm, order_hbm), (transfer_ref, basis_ref, order_ref), sems
    )
    device = device_ref[0]
    high, core = jnp.right_shift(device, LOW + 1), jnp.bitwise_and(device, 1)
    total = mm(
        unpacked([received_ref[2 * g] + received_ref[2 * g + 1] for g in range(NHIGH)]),
        weight_ref[...].reshape(NHIGH * RANK, 2 * RANK),
    )
    total = total[:COLS] + total[COLS:]
    sibling = received_ref[high * 2 + 1 - core]
    field = field_ref[...] + (total[:, :RANK] + total[:, RANK:])
    field = field + jnp.concatenate([sibling[:, :RANK], sibling[:, RANK:]], axis=0)
    hi, lo = halves(field)
    for copy in copies:
        copy.wait()
    fields = mm_nt(
        jnp.concatenate([hi, lo], axis=0), transfer_ref[...].reshape(LEAVES * RANK, RANK)
    )
    hi, lo = halves(fields[:COLS] + fields[COLS:])
    both = jnp.concatenate([hi, lo], axis=0)
    values = [mm(both[:, n * RANK : (n + 1) * RANK], basis_ref[n]) for n in range(LEAVES)]
    values = jnp.concatenate([v[:COLS] + v[COLS:] for v in values], axis=1) + partial_ref[...]
    hi, lo = halves(values)
    both = jnp.concatenate([hi, lo], axis=0)
    order = order_ref[...]
    block = jnp.right_shift(order, 8)
    masked = [both * jnp.where(block == h, 1.0, 0.0).astype(BF) for h in range(BLOCKS)]
    result = mm_nt(jnp.concatenate(masked, axis=0), low_onehot(order))
    for h in range(BLOCKS):
        at = h * 2 * COLS
        out_ref[:, h * WIDE : (h + 1) * WIDE] = result[at : at + COLS] + result[at + COLS : at + 2 * COLS]


def call(kernel, out, inputs, buffers=(), scratch=(), flops=0, transcendentals=0, vmem=16):
    shapes = [jax.ShapeDtypeStruct(s, t) for s, t in out]
    scratches = [pltpu.VMEM(s, t) for s, t in buffers] + [pltpu.VMEM(s, t) for s, t in scratch]
    if buffers:
        scratches.append(pltpu.SemaphoreType.DMA((len(buffers),)))
    return pl.pallas_call(
        kernel,
        out_shape=shapes,
        in_specs=[space for space, _ in inputs],
        out_specs=[VMEM] * len(out),
        scratch_shapes=scratches,
        compiler_params=pltpu.CompilerParams(vmem_limit_bytes=vmem << 20),
        cost_estimate=pl.CostEstimate(
            flops=flops, bytes_accessed=1 << 20, transcendentals=transcendentals
        ),
    )(*[array for _, array in inputs])


def per_device(
    right_sides,
    coordinates,
    tree_order,
    leaf_basis,
    far_pairs,
    far_coupling,
    near_pairs,
    leaf_transfer,
    top_transfer,
    top_coupling,
):
    count = lax.axis_size("leaf")
    device = lax.axis_index("leaf").astype(jnp.int32).reshape(1)
    order = tree_order.reshape(1, PTS)
    basis_like = (leaf_basis.shape, BF)
    transfer_like = (leaf_transfer.shape, BF)
    order_like = (order.shape, jnp.int32)
    sorted_rhs, coef, message = call(
        up_kernel,
        [((COLS, PTS), BF), ((LEAVES, COLS, RANK), F32), ((NLOW, 8, 2 * RANK), F32)],
        [(HBM, order), (HBM, right_sides), (HBM, leaf_basis), (HBM, leaf_transfer)],
        buffers=[order_like, (right_sides.shape, F32), basis_like, transfer_like],
        vmem=62,
        flops=1 << 28,
    )
    low_groups = [
        [(g * NLOW + z) * 2 + c for z in range(NLOW)] for g in range(NHIGH) for c in range(2)
    ]
    high_groups = [
        [(g * NLOW + z) * 2 + c for g in range(NHIGH) for c in range(2)] for z in range(NLOW)
    ]
    received = lax.all_to_all(message, "leaf", 0, 0, axis_index_groups=low_groups, tiled=True)

    inner, across, points = call(
        points_kernel,
        [((2 * COLS, LEAF), BF), ((2 * COLS, LEAF), BF), ((COLS, PTS), BF)],
        [(SMEM, device), (HBM, coordinates), (HBM, order), (VMEM, sorted_rhs)],
        buffers=[(coordinates.shape, BF), order_like],
        flops=1 << 28,
    )
    inner = lax.ppermute(inner, "leaf", [(i, i ^ 1) for i in range(count)])
    pairs = [(i, i + 1) for i in range(1, count - 1, 2)]
    across = lax.ppermute(across, "leaf", pairs + [(j, i) for i, j in pairs])
    low_weight, high_weight = call(
        weights_kernel,
        [((NLOW, RANK, 6 * RANK), BF), ((NHIGH, RANK, 2 * RANK), BF)],
        [(SMEM, device), (HBM, top_transfer), (HBM, top_coupling)],
        buffers=[(top_transfer.shape, BF), (top_coupling.shape, BF)],
        flops=1 << 30,
    )
    message, field = call(
        middle_kernel,
        [((2 * NHIGH, 8, 2 * RANK), F32), ((COLS, RANK), F32)],
        [(SMEM, device), (VMEM, received), (VMEM, low_weight)],
        flops=1 << 27,
    )
    received = lax.all_to_all(message, "leaf", 0, 0, axis_index_groups=high_groups, tiled=True)
    coupling = far_coupling.transpose(1, 2, 0)
    (partial,) = call(
        local_kernel,
        [((COLS, PTS), F32)],
        [
            (SMEM, device),
            (SMEM, near_pairs),
            (SMEM, far_pairs),
            (ANY, field),
            (VMEM, coef),
            (VMEM, coupling),
            (VMEM, leaf_basis),
            (VMEM, sorted_rhs),
            (VMEM, points),
            (VMEM, inner),
            (VMEM, across),
        ],
        scratch=[
            ((LEAF * RANK // 2, 2 * RANK), F32),
            ((LEAVES, 4 * COLS, 2 * RANK), BF),
            ((LEAVES, RANK // 2, 4 * COLS), F32),
            ((LEAVES + 2, COLS, LEAF), BF),
            ((LEAVES + 2, LEAF, COLS), BF),
            ((LEAVES + 2, COLS, LEAF), BF),
            ((LEAVES, COLS, LEAF), F32),
        ],
        flops=1 << 32,
        transcendentals=1 << 21,
    )
    (product,) = call(
        down_kernel,
        [((COLS, PTS), F32)],
        [
            (SMEM, device),
            (VMEM, received),
            (VMEM, high_weight),
            (VMEM, field),
            (VMEM, partial),
            (HBM, leaf_transfer),
            (HBM, leaf_basis),
            (HBM, order),
        ],
        buffers=[transfer_like, basis_like, order_like],
        flops=1 << 28,
    )
    return product


def solution(mesh):
    return jax.shard_map(
        per_device,
        mesh=mesh,
        in_specs=(
            P(None, "leaf"),
            P(None, "leaf"),
            P("leaf"),
            P("leaf", None, None),
            P(None, "leaf"),
            P("leaf", None, None),
            P(None, "leaf"),
            P("leaf", None, None),
            P(),
            P(),
        ),
        out_specs=P(None, "leaf"),
        check_vma=False,
    )
```

```python
import jax
import jax.numpy as jnp
from jax import lax
from jax.experimental import pallas as pl
from jax.experimental.pallas import tpu as pltpu
from jax.sharding import PartitionSpec as P

BF = jnp.bfloat16
F32 = jnp.float32
LEAF = 128
RANK = 64
COLS = 16
LEAVES = 16
WIDE = 256
BLOCKS = 8
PTS = LEAVES * LEAF
LOW = 4
HIGHS = 4
WEIGHTS_FIRST = 4
LEADER = 10
MIDDLE = 9
NLOW = 1 << LOW
NHIGH = 1 << HIGHS
LOG2E = 1.4426950408889634
VMEM = pl.BlockSpec(memory_space=pltpu.VMEM)
SMEM = pl.BlockSpec(memory_space=pltpu.SMEM)
ANY = pl.BlockSpec(memory_space=pl.ANY)
HBM = pl.BlockSpec(memory_space=pltpu.HBM)


def halves(x):
    hi = x.astype(BF)
    return hi, (x - hi.astype(F32)).astype(BF)


def mm(a, b):
    return jnp.dot(a, b, preferred_element_type=F32)


def mm_nt(a, b):
    return lax.dot_general(a, b, (((1,), (1,)), ((), ())), preferred_element_type=F32)


def wide(a, b):
    ah, al = halves(a)
    bh, bl = halves(b)
    return mm(ah, bh) + (mm(ah, bl) + mm(al, bh))


def wide_nt(a, b):
    ah, al = halves(a)
    bh, bl = halves(b)
    return mm_nt(ah, bh) + (mm_nt(ah, bl) + mm_nt(al, bh))


def low_onehot(order):
    lane = jnp.bitwise_and(order, WIDE - 1).astype(F32).astype(BF)
    rows = lax.broadcasted_iota(jnp.int32, (WIDE, order.shape[1]), 0).astype(F32).astype(BF)
    return jnp.where(rows == lane, jnp.ones((), BF), jnp.zeros((), BF))


def permuted(x, order, width):
    stacked = jnp.concatenate([x[:, h * WIDE : (h + 1) * WIDE] for h in range(BLOCKS)], axis=0)
    rows = x.shape[0]
    for start in range(0, order.shape[1], width):
        piece = order[:, start : start + width]
        picked = mm(stacked, low_onehot(piece))
        block = jnp.right_shift(piece, 8)
        total = jnp.zeros((rows, width), F32)
        for h in range(BLOCKS):
            total = total + jnp.where(block == h, picked[h * rows : (h + 1) * rows], 0.0)
        yield start, total.astype(BF)


def pack_message(x):
    return jnp.concatenate([x[:8], x[8:]], axis=1)


def fetch(sources, buffers, sems):
    copies = [
        pltpu.make_async_copy(source, buffer, sems.at[i])
        for i, (source, buffer) in enumerate(zip(sources, buffers, strict=True))
    ]
    for copy in copies:
        copy.start()
    return copies


def along_z(device):
    return jnp.bitwise_and(jnp.right_shift(device, 1), NLOW - 1)


def weights_first(device):
    return jnp.logical_and(along_z(device) < WEIGHTS_FIRST, device != 0)


def up_kernel(
    order_hbm, rhs_hbm, basis_hbm, transfer_hbm, top_transfer_hbm, top_coupling_hbm,
    sorted_ref, coef_ref, message_ref, low_hbm, high_hbm,
    order_ref, rhs_ref, basis_ref, transfer_ref, top_transfer_ref, top_coupling_ref, low_ref, high_ref, sems
):
    device = lax.axis_index("leaf")
    copies = fetch(
        (order_hbm, rhs_hbm, basis_hbm, transfer_hbm),
        (order_ref, rhs_ref, basis_ref, transfer_ref),
        sems,
    )
    copies[0].wait()
    copies[1].wait()
    x = rhs_ref[...].astype(BF)
    order = order_ref[...]
    block = jnp.right_shift(order, 8)
    places = low_onehot(order)
    copies[2].wait()
    copies[3].wait()
    stacked = jnp.concatenate([x[:, h * WIDE : (h + 1) * WIDE] for h in range(BLOCKS)], axis=0)
    picked = mm(stacked, places)
    total = jnp.where(block == 0, picked[:COLS], 0.0)
    for h in range(1, BLOCKS):
        total = total + jnp.where(block == h, picked[h * COLS : (h + 1) * COLS], 0.0)
    total = total.astype(BF)
    sorted_ref[...] = total
    coefs = []
    for n in range(LEAVES):
        coef = mm_nt(total[:, n * LEAF : (n + 1) * LEAF], basis_ref[n])
        coefs.append(coef)
        coef_ref[n] = coef
    hi, lo = halves(jnp.concatenate(coefs, axis=1))
    root = mm(jnp.concatenate([hi, lo], axis=0), transfer_ref[...].reshape(LEAVES * RANK, RANK))
    message = pack_message(root[:COLS] + root[COLS:])
    message_ref[...] = jnp.broadcast_to(message[None], message_ref.shape)

    @pl.when(weights_first(device))
    def _():
        for copy in fetch(
            (top_transfer_hbm, top_coupling_hbm), (top_transfer_ref, top_coupling_ref), sems
        ):
            copy.wait()
        form_weights(device, top_transfer_ref, top_coupling_ref, low_ref, high_ref)
        for copy in fetch((low_ref, high_ref), (low_hbm, high_hbm), sems):
            copy.wait()


def points_kernel(coords_hbm, order_hbm, sorted_ref, near_ref, across_ref, points_ref, coords_ref, order_ref, sems):
    copies = fetch((coords_hbm, order_hbm), (coords_ref, order_ref), sems)
    for copy in copies:
        copy.wait()
    x = jnp.concatenate([coords_ref[...], jnp.zeros((13, PTS), BF)], axis=0)
    for start, piece in permuted(x, order_ref[...], 2 * LEAF):
        points_ref[:, start : start + 2 * LEAF] = piece
    head = jnp.concatenate([sorted_ref[:, 0:LEAF], points_ref[:, 0:LEAF]], axis=0)
    tail = jnp.concatenate([sorted_ref[:, PTS - LEAF :], points_ref[:, PTS - LEAF :]], axis=0)
    even = jnp.bitwise_and(lax.axis_index("leaf"), 1) == 0

    @pl.when(even)
    def _():
        near_ref[...] = tail
        across_ref[...] = head

    @pl.when(jnp.logical_not(even))
    def _():
        near_ref[...] = head
        across_ref[...] = tail


def point_features(points):
    p = points.astype(F32)
    x, y, z = p[0:1], p[1:2], p[2:3]
    square = x * x + y * y + z * z
    s0 = square.astype(BF).astype(F32)
    rest = square - s0
    s1 = rest.astype(BF).astype(F32)
    s2 = rest - s1
    one = jnp.ones_like(square)
    zero = jnp.zeros((7, points.shape[1]), F32)
    source = jnp.concatenate([x, y, z, one, one, one, s0, s1, s2, zero], axis=0)
    target = jnp.concatenate(
        [-2.0 * x, -2.0 * y, -2.0 * z, s0, s1, s2, one, one, one, zero], axis=0
    )
    return source, target


def local_kernel(
    near_ref, far_ref, after_ref, coef_ref, coupling_ref, basis_ref, sorted_ref, points_ref, inner_ref, across_ref, out_ref,
    by_pair, spread, far, rhs, source, target, near
):
    del after_ref
    rows = lax.broadcasted_iota(jnp.int32, (LEAF, LEAF), 0)
    columns = lax.broadcasted_iota(jnp.int32, (LEAF, LEAF), 1)
    identity = jnp.where(rows == columns, 1.0, 0.0).astype(BF)
    for a in range(RANK // 2):
        two = jnp.concatenate([coupling_ref[a], coupling_ref[a + RANK // 2]], axis=0)
        by_pair[a * LEAF : (a + 1) * LEAF, :] = mm_nt(identity, two)
    zero = jnp.zeros((2 * COLS, RANK), BF)
    for n in range(LEAVES):
        hi, lo = halves(coef_ref[n])
        both = jnp.concatenate([hi, lo], axis=0)
        spread[n] = jnp.concatenate(
            [jnp.concatenate([both, zero], axis=1), jnp.concatenate([zero, both], axis=1)], axis=0
        )
    far[...] = jnp.zeros_like(far)
    near[...] = jnp.zeros_like(near)

    even = jnp.bitwise_and(lax.axis_index("leaf"), 1) == 0
    inner, across = inner_ref[...].astype(F32), across_ref[...].astype(F32)
    left = jnp.where(even, across, inner).astype(BF)
    right = jnp.where(even, inner, across).astype(BF)
    columns = jnp.concatenate([left[:COLS], sorted_ref[...], right[:COLS]], axis=1)
    points = jnp.concatenate([left[COLS:], points_ref[...], right[COLS:]], axis=1)
    of_source, of_target = point_features(points)
    of_target = of_target.astype(BF)
    for n in range(LEAVES + 2):
        here = slice(n * LEAF, (n + 1) * LEAF)
        rhs[n] = columns[:, here]
        source[n] = of_source[:, here].T.astype(BF)
        target[n] = of_target[:, here]

    def far_pair(j):
        to, of = far_ref[0, j], far_ref[1, j]
        rows = by_pair[pl.ds(j, RANK // 2, stride=LEAF), :].astype(BF)
        far[to] += mm_nt(rows, spread[of])

    def near_pair(j):
        to, of = near_ref[0, j], near_ref[1, j]
        squared = jnp.maximum(mm(source[of], target[to + 1]) * (3.0 * LOG2E * LOG2E), 1e-30)
        scaled = squared * lax.rsqrt(squared)
        values = ((0.125 + (0.125 / LOG2E) * scaled) * jnp.exp2(-scaled)).astype(BF)
        near[to] += mm(rhs[of], values)

    for j in range(8 * LEAVES):
        far_pair(j)
    for j in range(3 * LEAVES):
        near_pair(j)
    for n in range(LEAVES):
        x = far[n].T
        field = jnp.concatenate(
            [x[:COLS] + x[COLS : 2 * COLS], x[2 * COLS : 3 * COLS] + x[3 * COLS :]], axis=1
        )
        hi, lo = halves(field)
        both = mm(jnp.concatenate([hi, lo], axis=0), basis_ref[n])
        out_ref[:, n * LEAF : (n + 1) * LEAF] = near[n] + (both[:COLS] + both[COLS:])


def times(a, b):
    hi, lo = halves(a)
    both = mm(jnp.concatenate([hi, lo], axis=0), b)
    return both[: a.shape[0]] + both[a.shape[0] :]


def weights_kernel(transfer_ref, coupling_ref, low_ref, high_ref):
    device = lax.axis_index("leaf")

    @pl.when(jnp.logical_not(weights_first(device)))
    def _():
        form_weights(device, transfer_ref, coupling_ref, low_ref, high_ref)


def form_weights(device, transfer_ref, coupling_ref, low_ref, high_ref):
    core = jnp.bitwise_and(device, 1)
    low = along_z(device)
    high = jnp.right_shift(device, LOW + 1)
    mine, other = transfer_ref[0, core], transfer_ref[0, 1 - core]

    hi, lo = halves(coupling_ref[0, 1 - core].astype(F32).T)
    zero = jnp.zeros((RANK, RANK), BF)
    low_ref[pl.ds(low, 1), :, 2 * RANK :] = jnp.concatenate([zero, hi, zero, lo], axis=1)[None]

    senders = mine.astype(F32)
    path = jnp.concatenate([mine, other], axis=0).astype(F32)
    for level in range(1, LOW + 1):
        h = level - 1
        node = jnp.right_shift(low, h)
        side = jnp.bitwise_and(node, 1)
        at = jnp.left_shift(jnp.bitwise_xor(node, 1), h)
        end = times(path, coupling_ref[level, side])
        hi, lo = halves(wide_nt(senders, end))
        low_ref[pl.ds(at, 1 << h), :, 2 * RANK :] = jnp.concatenate([hi, lo], axis=1).reshape(
            1 << h, RANK, 4 * RANK
        )
        path = times(path, transfer_ref[level, side])
        senders = jnp.concatenate(
            [times(senders, transfer_ref[level, 0]), times(senders, transfer_ref[level, 1])], axis=0
        )
    hi, lo = halves(senders)
    low_ref[:, :, : 2 * RANK] = jnp.concatenate([hi, lo], axis=1).reshape(NLOW, RANK, 2 * RANK)

    path = path[:RANK]
    high_ref[pl.ds(high, 1)] = jnp.zeros((1, RANK, 2 * RANK), BF)
    for h in range(HIGHS):
        level = LOW + 1 + h
        node = jnp.right_shift(high, h)
        side = jnp.bitwise_and(node, 1)
        at = jnp.left_shift(jnp.bitwise_xor(node, 1), h)
        end = times(path, coupling_ref[level, side])
        hi, lo = halves(end.T if h == 0 else wide_nt(senders, end))
        high_ref[pl.ds(at, 1 << h)] = jnp.concatenate([hi, lo], axis=1).reshape(
            1 << h, RANK, 2 * RANK
        )
        if h == HIGHS - 1:
            break
        path = times(path, transfer_ref[level, side])
        if h == 0:
            senders = transfer_ref[level].reshape(2 * RANK, RANK).astype(F32)
        else:
            senders = jnp.concatenate(
                [times(senders, transfer_ref[level, 0]), times(senders, transfer_ref[level, 1])], axis=0
            )


def unpacked(messages):
    x = jnp.concatenate([m[:, :RANK] for m in messages], axis=1)
    y = jnp.concatenate([m[:, RANK:] for m in messages], axis=1)
    hi, lo = halves(jnp.concatenate([x, y], axis=0))
    return jnp.concatenate([hi, lo], axis=0)


def middle_kernel(received_ref, early_ref, late_ref, message_ref, field_ref):
    device = lax.axis_index("leaf")
    weight = jnp.where(weights_first(device), early_ref[...], late_ref[...])
    total = mm(
        unpacked([received_ref[(z - LEADER) % NLOW] for z in range(NLOW)]), weight.reshape(NLOW * RANK, 6 * RANK)
    )
    total = total[:COLS] + total[COLS:]
    node = total[:, :RANK] + total[:, RANK : 2 * RANK]
    fields = total[:, 2 * RANK : 4 * RANK] + total[:, 4 * RANK :]
    field_ref[...] = fields[:, :RANK]
    message_ref[...] = jnp.broadcast_to(pack_message(node)[None], message_ref.shape)
    high, core = jnp.right_shift(device, LOW + 1), jnp.bitwise_and(device, 1)
    at = jnp.bitwise_and(high - MIDDLE, NHIGH - 1)
    message_ref[at * 2 + 1 - core] = pack_message(fields[:, RANK:])


def down_kernel(
    received_ref, early_ref, late_ref, field_ref, partial_ref, transfer_hbm, basis_hbm, order_hbm, out_ref, transfer_ref, basis_ref, order_ref, sems
):
    copies = fetch(
        (transfer_hbm, basis_hbm, order_hbm), (transfer_ref, basis_ref, order_ref), sems
    )
    device = lax.axis_index("leaf")
    high, core = jnp.right_shift(device, LOW + 1), jnp.bitwise_and(device, 1)
    places = [(g - MIDDLE) % NHIGH for g in range(NHIGH)]
    total = mm(
        unpacked([received_ref[2 * g] + received_ref[2 * g + 1] for g in places]),
        jnp.where(weights_first(device), early_ref[...], late_ref[...]).reshape(NHIGH * RANK, 2 * RANK),
    )
    total = total[:COLS] + total[COLS:]
    sibling = received_ref[jnp.bitwise_and(high - MIDDLE, NHIGH - 1) * 2 + 1 - core]
    field = field_ref[...] + (total[:, :RANK] + total[:, RANK:])
    field = field + jnp.concatenate([sibling[:, :RANK], sibling[:, RANK:]], axis=0)
    hi, lo = halves(field)
    for copy in copies:
        copy.wait()
    fields = mm_nt(
        jnp.concatenate([hi, lo], axis=0), transfer_ref[...].reshape(LEAVES * RANK, RANK)
    )
    hi, lo = halves(fields[:COLS] + fields[COLS:])
    both = jnp.concatenate([hi, lo], axis=0)
    values = [mm(both[:, n * RANK : (n + 1) * RANK], basis_ref[n]) for n in range(LEAVES)]
    values = jnp.concatenate([v[:COLS] + v[COLS:] for v in values], axis=1) + partial_ref[...]
    hi, lo = halves(values)
    both = jnp.concatenate([hi, lo], axis=0)
    order = order_ref[...]
    block = jnp.right_shift(order, 8)
    masked = [both * jnp.where(block == h, 1.0, 0.0).astype(BF) for h in range(BLOCKS)]
    result = mm_nt(jnp.concatenate(masked, axis=0), low_onehot(order))
    for h in range(BLOCKS):
        at = h * 2 * COLS
        out_ref[:, h * WIDE : (h + 1) * WIDE] = result[at : at + COLS] + result[at + COLS : at + 2 * COLS]


def call(kernel, out, inputs, buffers=(), scratch=(), flops=0, transcendentals=0, vmem=16):
    shapes = [jax.ShapeDtypeStruct(o[0], o[1]) for o in out]
    scratches = [pltpu.VMEM(s, t) for s, t in buffers] + [pltpu.VMEM(s, t) for s, t in scratch]
    if buffers:
        scratches.append(pltpu.SemaphoreType.DMA((len(buffers),)))
    return pl.pallas_call(
        kernel,
        out_shape=shapes,
        in_specs=[space for space, _ in inputs],
        out_specs=[o[2] if len(o) > 2 else VMEM for o in out],
        scratch_shapes=scratches,
        compiler_params=pltpu.CompilerParams(vmem_limit_bytes=vmem << 20),
        cost_estimate=pl.CostEstimate(
            flops=flops, bytes_accessed=1 << 20, transcendentals=transcendentals
        ),
    )(*[array for _, array in inputs])


def per_device(
    right_sides,
    coordinates,
    tree_order,
    leaf_basis,
    far_pairs,
    far_coupling,
    near_pairs,
    leaf_transfer,
    top_transfer,
    top_coupling,
):
    count = lax.axis_size("leaf")
    order = tree_order.reshape(1, PTS)
    basis_like = (leaf_basis.shape, BF)
    transfer_like = (leaf_transfer.shape, BF)
    order_like = (order.shape, jnp.int32)
    low_like = ((NLOW, RANK, 6 * RANK), BF)
    high_like = ((NHIGH, RANK, 2 * RANK), BF)
    top_like = (top_transfer.shape, BF)
    sorted_rhs, coef, message, early_low, early_high = call(
        up_kernel,
        [
            ((COLS, PTS), BF),
            ((LEAVES, COLS, RANK), F32),
            ((NLOW, 8, 2 * RANK), F32),
            (*low_like, HBM),
            (*high_like, HBM),
        ],
        [
            (HBM, array)
            for array in (order, right_sides, leaf_basis, leaf_transfer, top_transfer, top_coupling)
        ],
        buffers=[order_like, (right_sides.shape, F32), basis_like, transfer_like]
        + [top_like, top_like, low_like, high_like],
        vmem=62,
        flops=1 << 28,
    )
    low_groups = [
        [(g * NLOW + (LEADER + z) % NLOW) * 2 + c for z in range(NLOW)]
        for g in range(NHIGH)
        for c in range(2)
    ]
    high_groups = [
        [((MIDDLE + g) % NHIGH * NLOW + z) * 2 + c for g in range(NHIGH) for c in range(2)]
        for z in range(NLOW)
    ]
    received = lax.all_to_all(message, "leaf", 0, 0, axis_index_groups=low_groups, tiled=True)

    inner, across, points = call(
        points_kernel,
        [((2 * COLS, LEAF), BF), ((2 * COLS, LEAF), BF), ((COLS, PTS), BF)],
        [(HBM, coordinates), (HBM, order), (VMEM, sorted_rhs)],
        buffers=[(coordinates.shape, BF), order_like],
        flops=1 << 28,
    )
    inner = lax.ppermute(inner, "leaf", [(i, i ^ 1) for i in range(count)])
    pairs = [(i, i + 1) for i in range(1, count - 1, 2)]
    across = lax.ppermute(across, "leaf", pairs + [(j, i) for i, j in pairs])
    late_low, late_high = call(
        weights_kernel,
        [low_like, high_like],
        [(VMEM, top_transfer), (VMEM, top_coupling)],
        flops=1 << 30,
    )
    message, field = call(
        middle_kernel,
        [((2 * NHIGH, 8, 2 * RANK), F32), ((COLS, RANK), F32)],
        [(VMEM, received), (VMEM, early_low), (VMEM, late_low)],
        flops=1 << 27,
    )
    received = lax.all_to_all(message, "leaf", 0, 0, axis_index_groups=high_groups, tiled=True)
    coupling = far_coupling.transpose(1, 2, 0)
    (partial,) = call(
        local_kernel,
        [((COLS, PTS), F32)],
        [
            (SMEM, near_pairs),
            (SMEM, far_pairs),
            (ANY, field),
            (VMEM, coef),
            (VMEM, coupling),
            (VMEM, leaf_basis),
            (VMEM, sorted_rhs),
            (VMEM, points),
            (VMEM, inner),
            (VMEM, across),
        ],
        scratch=[
            ((LEAF * RANK // 2, 2 * RANK), F32),
            ((LEAVES, 4 * COLS, 2 * RANK), BF),
            ((LEAVES, RANK // 2, 4 * COLS), F32),
            ((LEAVES + 2, COLS, LEAF), BF),
            ((LEAVES + 2, LEAF, COLS), BF),
            ((LEAVES + 2, COLS, LEAF), BF),
            ((LEAVES, COLS, LEAF), F32),
        ],
        flops=1 << 32,
        transcendentals=1 << 21,
    )
    (product,) = call(
        down_kernel,
        [((COLS, PTS), F32)],
        [
            (VMEM, received),
            (VMEM, early_high),
            (VMEM, late_high),
            (VMEM, field),
            (VMEM, partial),
            (HBM, leaf_transfer),
            (HBM, leaf_basis),
            (HBM, order),
        ],
        buffers=[transfer_like, basis_like, order_like],
        flops=1 << 28,
    )
    return product


def solution(mesh):
    return jax.shard_map(
        per_device,
        mesh=mesh,
        in_specs=(
            P(None, "leaf"),
            P(None, "leaf"),
            P("leaf"),
            P("leaf", None, None),
            P(None, "leaf"),
            P("leaf", None, None),
            P(None, "leaf"),
            P("leaf", None, None),
            P(),
            P(),
        ),
        out_specs=P(None, "leaf"),
        check_vma=False,
    )
```

```python
import jax
import jax.numpy as jnp
from jax import lax
from jax.experimental import pallas as pl
from jax.experimental.pallas import tpu as pltpu
from jax.sharding import PartitionSpec as P

BF = jnp.bfloat16
F32 = jnp.float32
LEAF = 128
RANK = 64
COLS = 16
LEAVES = 16
WIDE = 256
BLOCKS = 8
PTS = LEAVES * LEAF
LOW = 4
HIGHS = 4
WEIGHTS_FIRST = 3
LEADER = 11
MIDDLE = 9
NLOW = 1 << LOW
NHIGH = 1 << HIGHS
LOG2E = 1.4426950408889634
VMEM = pl.BlockSpec(memory_space=pltpu.VMEM)
SMEM = pl.BlockSpec(memory_space=pltpu.SMEM)
ANY = pl.BlockSpec(memory_space=pl.ANY)
HBM = pl.BlockSpec(memory_space=pltpu.HBM)


def halves(x):
    hi = x.astype(BF)
    return hi, (x - hi.astype(F32)).astype(BF)


def mm(a, b):
    return jnp.dot(a, b, preferred_element_type=F32)


def mm_nt(a, b):
    return lax.dot_general(a, b, (((1,), (1,)), ((), ())), preferred_element_type=F32)


def wide(a, b):
    ah, al = halves(a)
    bh, bl = halves(b)
    return mm(ah, bh) + (mm(ah, bl) + mm(al, bh))


def wide_nt(a, b):
    ah, al = halves(a)
    bh, bl = halves(b)
    return mm_nt(ah, bh) + (mm_nt(ah, bl) + mm_nt(al, bh))


def low_onehot(order):
    lane = jnp.bitwise_and(order, WIDE - 1).astype(F32).astype(BF)
    rows = lax.broadcasted_iota(jnp.int32, (WIDE, order.shape[1]), 0).astype(F32).astype(BF)
    return jnp.where(rows == lane, jnp.ones((), BF), jnp.zeros((), BF))


def permuted(x, order, width):
    stacked = jnp.concatenate([x[:, h * WIDE : (h + 1) * WIDE] for h in range(BLOCKS)], axis=0)
    rows = x.shape[0]
    for start in range(0, order.shape[1], width):
        piece = order[:, start : start + width]
        picked = mm(stacked, low_onehot(piece))
        block = jnp.right_shift(piece, 8)
        total = jnp.zeros((rows, width), F32)
        for h in range(BLOCKS):
            total = total + jnp.where(block == h, picked[h * rows : (h + 1) * rows], 0.0)
        yield start, total.astype(BF)


def pack_message(x):
    return jnp.concatenate([x[:8], x[8:]], axis=1)


def fetch(sources, buffers, sems):
    copies = [
        pltpu.make_async_copy(source, buffer, sems.at[i])
        for i, (source, buffer) in enumerate(zip(sources, buffers, strict=True))
    ]
    for copy in copies:
        copy.start()
    return copies


def along_z(device):
    return jnp.bitwise_and(jnp.right_shift(device, 1), NLOW - 1)


def weights_first(device):
    return jnp.logical_and(along_z(device) < WEIGHTS_FIRST, device != 0)


def up_kernel(
    order_hbm, rhs_hbm, basis_hbm, transfer_hbm, top_transfer_hbm, top_coupling_hbm,
    sorted_ref, coef_ref, message_ref, low_hbm, high_hbm,
    order_ref, rhs_ref, basis_ref, transfer_ref, top_transfer_ref, top_coupling_ref, low_ref, high_ref, sems
):
    device = lax.axis_index("leaf")
    copies = fetch(
        (order_hbm, rhs_hbm, basis_hbm, transfer_hbm),
        (order_ref, rhs_ref, basis_ref, transfer_ref),
        sems,
    )
    copies[0].wait()
    copies[1].wait()
    x = rhs_ref[...].astype(BF)
    order = order_ref[...]
    block = jnp.right_shift(order, 8)
    places = low_onehot(order)
    copies[2].wait()
    copies[3].wait()
    stacked = jnp.concatenate([x[:, h * WIDE : (h + 1) * WIDE] for h in range(BLOCKS)], axis=0)
    picked = mm(stacked, places)
    total = jnp.where(block == 0, picked[:COLS], 0.0)
    for h in range(1, BLOCKS):
        total = total + jnp.where(block == h, picked[h * COLS : (h + 1) * COLS], 0.0)
    total = total.astype(BF)
    sorted_ref[...] = total
    coefs = []
    for n in range(LEAVES):
        coef = mm_nt(total[:, n * LEAF : (n + 1) * LEAF], basis_ref[n])
        coefs.append(coef)
        coef_ref[n] = coef
    hi, lo = halves(jnp.concatenate(coefs, axis=1))
    root = mm(jnp.concatenate([hi, lo], axis=0), transfer_ref[...].reshape(LEAVES * RANK, RANK))
    message = pack_message(root[:COLS] + root[COLS:])
    message_ref[...] = jnp.broadcast_to(message[None], message_ref.shape)

    @pl.when(weights_first(device))
    def _():
        for copy in fetch(
            (top_transfer_hbm, top_coupling_hbm), (top_transfer_ref, top_coupling_ref), sems
        ):
            copy.wait()
        form_weights(device, top_transfer_ref, top_coupling_ref, low_ref, high_ref)
        for copy in fetch((low_ref, high_ref), (low_hbm, high_hbm), sems):
            copy.wait()


def points_kernel(coords_hbm, order_hbm, sorted_ref, near_ref, across_ref, points_ref, coords_ref, order_ref, sems):
    copies = fetch((coords_hbm, order_hbm), (coords_ref, order_ref), sems)
    for copy in copies:
        copy.wait()
    x = jnp.concatenate([coords_ref[...], jnp.zeros((13, PTS), BF)], axis=0)
    for start, piece in permuted(x, order_ref[...], 2 * LEAF):
        points_ref[:, start : start + 2 * LEAF] = piece
    head = jnp.concatenate([sorted_ref[:, 0:LEAF], points_ref[:, 0:LEAF]], axis=0)
    tail = jnp.concatenate([sorted_ref[:, PTS - LEAF :], points_ref[:, PTS - LEAF :]], axis=0)
    even = jnp.bitwise_and(lax.axis_index("leaf"), 1) == 0

    @pl.when(even)
    def _():
        near_ref[...] = tail
        across_ref[...] = head

    @pl.when(jnp.logical_not(even))
    def _():
        near_ref[...] = head
        across_ref[...] = tail


def point_features(points):
    p = points.astype(F32)
    x, y, z = p[0:1], p[1:2], p[2:3]
    square = x * x + y * y + z * z
    s0 = square.astype(BF).astype(F32)
    rest = square - s0
    s1 = rest.astype(BF).astype(F32)
    s2 = rest - s1
    one = jnp.ones_like(square)
    zero = jnp.zeros((7, points.shape[1]), F32)
    source = jnp.concatenate([x, y, z, one, one, one, s0, s1, s2, zero], axis=0)
    target = jnp.concatenate(
        [-2.0 * x, -2.0 * y, -2.0 * z, s0, s1, s2, one, one, one, zero], axis=0
    )
    return source, target


def local_kernel(
    near_ref, far_ref, after_ref, coef_ref, coupling_ref, basis_ref, sorted_ref, points_ref, inner_ref, across_ref, out_ref,
    by_pair, spread, far, rhs, source, target, near
):
    del after_ref
    rows = lax.broadcasted_iota(jnp.int32, (LEAF, LEAF), 0)
    columns = lax.broadcasted_iota(jnp.int32, (LEAF, LEAF), 1)
    identity = jnp.where(rows == columns, 1.0, 0.0).astype(BF)
    for a in range(RANK // 2):
        two = jnp.concatenate([coupling_ref[a], coupling_ref[a + RANK // 2]], axis=0)
        by_pair[a * LEAF : (a + 1) * LEAF, :] = mm_nt(identity, two)
    zero = jnp.zeros((2 * COLS, RANK), BF)
    for n in range(LEAVES):
        hi, lo = halves(coef_ref[n])
        both = jnp.concatenate([hi, lo], axis=0)
        spread[n] = jnp.concatenate(
            [jnp.concatenate([both, zero], axis=1), jnp.concatenate([zero, both], axis=1)], axis=0
        )
    far[...] = jnp.zeros_like(far)
    near[...] = jnp.zeros_like(near)

    even = jnp.bitwise_and(lax.axis_index("leaf"), 1) == 0
    inner, across = inner_ref[...].astype(F32), across_ref[...].astype(F32)
    left = jnp.where(even, across, inner).astype(BF)
    right = jnp.where(even, inner, across).astype(BF)
    columns = jnp.concatenate([left[:COLS], sorted_ref[...], right[:COLS]], axis=1)
    points = jnp.concatenate([left[COLS:], points_ref[...], right[COLS:]], axis=1)
    of_source, of_target = point_features(points)
    of_target = of_target.astype(BF)
    for n in range(LEAVES + 2):
        here = slice(n * LEAF, (n + 1) * LEAF)
        rhs[n] = columns[:, here]
        source[n] = of_source[:, here].T.astype(BF)
        target[n] = of_target[:, here]

    def far_pair(j):
        to, of = far_ref[0, j], far_ref[1, j]
        rows = by_pair[pl.ds(j, RANK // 2, stride=LEAF), :].astype(BF)
        far[to] += mm_nt(rows, spread[of])

    def near_pair(j):
        to, of = near_ref[0, j], near_ref[1, j]
        squared = jnp.maximum(mm(source[of], target[to + 1]) * (3.0 * LOG2E * LOG2E), 1e-30)
        scaled = squared * lax.rsqrt(squared)
        values = ((0.125 + (0.125 / LOG2E) * scaled) * jnp.exp2(-scaled)).astype(BF)
        near[to] += mm(rhs[of], values)

    for j in range(8 * LEAVES):
        far_pair(j)
    for j in range(3 * LEAVES):
        near_pair(j)
    for n in range(LEAVES):
        x = far[n].T
        field = jnp.concatenate(
            [x[:COLS] + x[COLS : 2 * COLS], x[2 * COLS : 3 * COLS] + x[3 * COLS :]], axis=1
        )
        hi, lo = halves(field)
        both = mm(jnp.concatenate([hi, lo], axis=0), basis_ref[n])
        out_ref[:, n * LEAF : (n + 1) * LEAF] = near[n] + (both[:COLS] + both[COLS:])


def times(a, b):
    hi, lo = halves(a)
    both = mm(jnp.concatenate([hi, lo], axis=0), b)
    return both[: a.shape[0]] + both[a.shape[0] :]


def weights_kernel(transfer_ref, coupling_ref, low_ref, high_ref):
    device = lax.axis_index("leaf")

    @pl.when(jnp.logical_not(weights_first(device)))
    def _():
        form_weights(device, transfer_ref, coupling_ref, low_ref, high_ref)


def form_weights(device, transfer_ref, coupling_ref, low_ref, high_ref):
    core = jnp.bitwise_and(device, 1)
    low = along_z(device)
    high = jnp.right_shift(device, LOW + 1)
    mine, other = transfer_ref[0, core], transfer_ref[0, 1 - core]

    hi, lo = halves(coupling_ref[0, 1 - core].astype(F32).T)
    zero = jnp.zeros((RANK, RANK), BF)
    low_ref[pl.ds(low, 1), :, 2 * RANK :] = jnp.concatenate([zero, hi, zero, lo], axis=1)[None]

    senders = mine.astype(F32)
    path = jnp.concatenate([mine, other], axis=0).astype(F32)
    for level in range(1, LOW + 1):
        h = level - 1
        node = jnp.right_shift(low, h)
        side = jnp.bitwise_and(node, 1)
        at = jnp.left_shift(jnp.bitwise_xor(node, 1), h)
        end = times(path, coupling_ref[level, side])
        hi, lo = halves(wide_nt(senders, end))
        low_ref[pl.ds(at, 1 << h), :, 2 * RANK :] = jnp.concatenate([hi, lo], axis=1).reshape(
            1 << h, RANK, 4 * RANK
        )
        path = times(path, transfer_ref[level, side])
        senders = jnp.concatenate(
            [times(senders, transfer_ref[level, 0]), times(senders, transfer_ref[level, 1])], axis=0
        )
    hi, lo = halves(senders)
    low_ref[:, :, : 2 * RANK] = jnp.concatenate([hi, lo], axis=1).reshape(NLOW, RANK, 2 * RANK)

    path = path[:RANK]
    high_ref[pl.ds(high, 1)] = jnp.zeros((1, RANK, 2 * RANK), BF)
    for h in range(HIGHS):
        level = LOW + 1 + h
        node = jnp.right_shift(high, h)
        side = jnp.bitwise_and(node, 1)
        at = jnp.left_shift(jnp.bitwise_xor(node, 1), h)
        end = times(path, coupling_ref[level, side])
        hi, lo = halves(end.T if h == 0 else wide_nt(senders, end))
        high_ref[pl.ds(at, 1 << h)] = jnp.concatenate([hi, lo], axis=1).reshape(
            1 << h, RANK, 2 * RANK
        )
        if h == HIGHS - 1:
            break
        path = times(path, transfer_ref[level, side])
        if h == 0:
            senders = transfer_ref[level].reshape(2 * RANK, RANK).astype(F32)
        else:
            senders = jnp.concatenate(
                [times(senders, transfer_ref[level, 0]), times(senders, transfer_ref[level, 1])], axis=0
            )


def unpacked(messages):
    x = jnp.concatenate([m[:, :RANK] for m in messages], axis=1)
    y = jnp.concatenate([m[:, RANK:] for m in messages], axis=1)
    hi, lo = halves(jnp.concatenate([x, y], axis=0))
    return jnp.concatenate([hi, lo], axis=0)


def middle_kernel(received_ref, early_ref, late_ref, message_ref, field_ref):
    device = lax.axis_index("leaf")
    weight = jnp.where(weights_first(device), early_ref[...], late_ref[...])
    total = mm(
        unpacked([received_ref[(z - LEADER) % NLOW] for z in range(NLOW)]), weight.reshape(NLOW * RANK, 6 * RANK)
    )
    total = total[:COLS] + total[COLS:]
    node = total[:, :RANK] + total[:, RANK : 2 * RANK]
    fields = total[:, 2 * RANK : 4 * RANK] + total[:, 4 * RANK :]
    field_ref[...] = fields[:, :RANK]
    message_ref[...] = jnp.broadcast_to(pack_message(node)[None], message_ref.shape)
    high, core = jnp.right_shift(device, LOW + 1), jnp.bitwise_and(device, 1)
    at = jnp.bitwise_and(high - MIDDLE, NHIGH - 1)
    message_ref[at * 2 + 1 - core] = pack_message(fields[:, RANK:])


def down_kernel(
    received_ref, early_ref, late_ref, field_ref, partial_ref, transfer_hbm, basis_hbm, order_hbm, out_ref, transfer_ref, basis_ref, order_ref, sems
):
    copies = fetch(
        (transfer_hbm, basis_hbm, order_hbm), (transfer_ref, basis_ref, order_ref), sems
    )
    device = lax.axis_index("leaf")
    high, core = jnp.right_shift(device, LOW + 1), jnp.bitwise_and(device, 1)
    places = [(g - MIDDLE) % NHIGH for g in range(NHIGH)]
    total = mm(
        unpacked([received_ref[2 * g] + received_ref[2 * g + 1] for g in places]),
        jnp.where(weights_first(device), early_ref[...], late_ref[...]).reshape(NHIGH * RANK, 2 * RANK),
    )
    total = total[:COLS] + total[COLS:]
    sibling = received_ref[jnp.bitwise_and(high - MIDDLE, NHIGH - 1) * 2 + 1 - core]
    field = field_ref[...] + (total[:, :RANK] + total[:, RANK:])
    field = field + jnp.concatenate([sibling[:, :RANK], sibling[:, RANK:]], axis=0)
    hi, lo = halves(field)
    for copy in copies:
        copy.wait()
    fields = mm_nt(
        jnp.concatenate([hi, lo], axis=0), transfer_ref[...].reshape(LEAVES * RANK, RANK)
    )
    hi, lo = halves(fields[:COLS] + fields[COLS:])
    both = jnp.concatenate([hi, lo], axis=0)
    values = [mm(both[:, n * RANK : (n + 1) * RANK], basis_ref[n]) for n in range(LEAVES)]
    values = jnp.concatenate([v[:COLS] + v[COLS:] for v in values], axis=1) + partial_ref[...]
    hi, lo = halves(values)
    both = jnp.concatenate([hi, lo], axis=0)
    order = order_ref[...]
    block = jnp.right_shift(order, 8)
    masked = [both * jnp.where(block == h, 1.0, 0.0).astype(BF) for h in range(BLOCKS)]
    result = mm_nt(jnp.concatenate(masked, axis=0), low_onehot(order))
    for h in range(BLOCKS):
        at = h * 2 * COLS
        out_ref[:, h * WIDE : (h + 1) * WIDE] = result[at : at + COLS] + result[at + COLS : at + 2 * COLS]


def call(kernel, out, inputs, buffers=(), scratch=(), flops=0, transcendentals=0, vmem=16):
    shapes = [jax.ShapeDtypeStruct(o[0], o[1]) for o in out]
    scratches = [pltpu.VMEM(s, t) for s, t in buffers] + [pltpu.VMEM(s, t) for s, t in scratch]
    if buffers:
        scratches.append(pltpu.SemaphoreType.DMA((len(buffers),)))
    return pl.pallas_call(
        kernel,
        out_shape=shapes,
        in_specs=[space for space, _ in inputs],
        out_specs=[o[2] if len(o) > 2 else VMEM for o in out],
        scratch_shapes=scratches,
        compiler_params=pltpu.CompilerParams(vmem_limit_bytes=vmem << 20),
        cost_estimate=pl.CostEstimate(
            flops=flops, bytes_accessed=1 << 20, transcendentals=transcendentals
        ),
    )(*[array for _, array in inputs])


def per_device(
    right_sides,
    coordinates,
    tree_order,
    leaf_basis,
    far_pairs,
    far_coupling,
    near_pairs,
    leaf_transfer,
    top_transfer,
    top_coupling,
):
    count = lax.axis_size("leaf")
    order = tree_order.reshape(1, PTS)
    basis_like = (leaf_basis.shape, BF)
    transfer_like = (leaf_transfer.shape, BF)
    order_like = (order.shape, jnp.int32)
    low_like = ((NLOW, RANK, 6 * RANK), BF)
    high_like = ((NHIGH, RANK, 2 * RANK), BF)
    top_like = (top_transfer.shape, BF)
    sorted_rhs, coef, message, early_low, early_high = call(
        up_kernel,
        [
            ((COLS, PTS), BF),
            ((LEAVES, COLS, RANK), F32),
            ((NLOW, 8, 2 * RANK), F32),
            (*low_like, HBM),
            (*high_like, HBM),
        ],
        [
            (HBM, array)
            for array in (order, right_sides, leaf_basis, leaf_transfer, top_transfer, top_coupling)
        ],
        buffers=[order_like, (right_sides.shape, F32), basis_like, transfer_like]
        + [top_like, top_like, low_like, high_like],
        vmem=62,
        flops=1 << 28,
    )
    low_groups = [
        [(g * NLOW + (LEADER + z) % NLOW) * 2 + c for z in range(NLOW)]
        for g in range(NHIGH)
        for c in range(2)
    ]
    high_groups = [
        [((MIDDLE + g) % NHIGH * NLOW + z) * 2 + c for g in range(NHIGH) for c in range(2)]
        for z in range(NLOW)
    ]
    received = lax.all_to_all(message, "leaf", 0, 0, axis_index_groups=low_groups, tiled=True)

    inner, across, points = call(
        points_kernel,
        [((2 * COLS, LEAF), BF), ((2 * COLS, LEAF), BF), ((COLS, PTS), BF)],
        [(HBM, coordinates), (HBM, order), (VMEM, sorted_rhs)],
        buffers=[(coordinates.shape, BF), order_like],
        flops=1 << 28,
    )
    inner = lax.ppermute(inner, "leaf", [(i, i ^ 1) for i in range(count)])
    pairs = [(i, i + 1) for i in range(1, count - 1, 2)]
    across = lax.ppermute(across, "leaf", pairs + [(j, i) for i, j in pairs])
    late_low, late_high = call(
        weights_kernel,
        [low_like, high_like],
        [(VMEM, top_transfer), (VMEM, top_coupling)],
        flops=1 << 30,
    )
    message, field = call(
        middle_kernel,
        [((2 * NHIGH, 8, 2 * RANK), F32), ((COLS, RANK), F32)],
        [(VMEM, received), (VMEM, early_low), (VMEM, late_low)],
        flops=1 << 27,
    )
    received = lax.all_to_all(message, "leaf", 0, 0, axis_index_groups=high_groups, tiled=True)
    coupling = far_coupling.transpose(1, 2, 0)
    (partial,) = call(
        local_kernel,
        [((COLS, PTS), F32)],
        [
            (SMEM, near_pairs),
            (SMEM, far_pairs),
            (ANY, field),
            (VMEM, coef),
            (VMEM, coupling),
            (VMEM, leaf_basis),
            (VMEM, sorted_rhs),
            (VMEM, points),
            (VMEM, inner),
            (VMEM, across),
        ],
        scratch=[
            ((LEAF * RANK // 2, 2 * RANK), F32),
            ((LEAVES, 4 * COLS, 2 * RANK), BF),
            ((LEAVES, RANK // 2, 4 * COLS), F32),
            ((LEAVES + 2, COLS, LEAF), BF),
            ((LEAVES + 2, LEAF, COLS), BF),
            ((LEAVES + 2, COLS, LEAF), BF),
            ((LEAVES, COLS, LEAF), F32),
        ],
        flops=1 << 32,
        transcendentals=1 << 21,
    )
    (product,) = call(
        down_kernel,
        [((COLS, PTS), F32)],
        [
            (VMEM, received),
            (VMEM, early_high),
            (VMEM, late_high),
            (VMEM, field),
            (VMEM, partial),
            (HBM, leaf_transfer),
            (HBM, leaf_basis),
            (HBM, order),
        ],
        buffers=[transfer_like, basis_like, order_like],
        flops=1 << 28,
    )
    return product


def solution(mesh):
    return jax.shard_map(
        per_device,
        mesh=mesh,
        in_specs=(
            P(None, "leaf"),
            P(None, "leaf"),
            P("leaf"),
            P("leaf", None, None),
            P(None, "leaf"),
            P("leaf", None, None),
            P(None, "leaf"),
            P("leaf", None, None),
            P(),
            P(),
        ),
        out_specs=P(None, "leaf"),
        check_vma=False,
    )
```

```python
import jax
import jax.numpy as jnp
from jax import lax
from jax.experimental import pallas as pl
from jax.experimental.pallas import tpu as pltpu
from jax.sharding import PartitionSpec as P

BF = jnp.bfloat16
F32 = jnp.float32
LEAF = 128
RANK = 64
COLS = 16
LEAVES = 16
WIDE = 256
BLOCKS = 8
PTS = LEAVES * LEAF
LOW = 4
HIGHS = 4
WEIGHTS_FIRST = 3
LEADER = 11
MIDDLE = 8
NLOW = 1 << LOW
NHIGH = 1 << HIGHS
LOG2E = 1.4426950408889634
VMEM = pl.BlockSpec(memory_space=pltpu.VMEM)
SMEM = pl.BlockSpec(memory_space=pltpu.SMEM)
ANY = pl.BlockSpec(memory_space=pl.ANY)
HBM = pl.BlockSpec(memory_space=pltpu.HBM)


def halves(x):
    hi = x.astype(BF)
    return hi, (x - hi.astype(F32)).astype(BF)


def mm(a, b):
    return jnp.dot(a, b, preferred_element_type=F32)


def mm_nt(a, b):
    return lax.dot_general(a, b, (((1,), (1,)), ((), ())), preferred_element_type=F32)


def wide(a, b):
    ah, al = halves(a)
    bh, bl = halves(b)
    return mm(ah, bh) + (mm(ah, bl) + mm(al, bh))


def wide_nt(a, b):
    ah, al = halves(a)
    bh, bl = halves(b)
    return mm_nt(ah, bh) + (mm_nt(ah, bl) + mm_nt(al, bh))


def low_onehot(order):
    lane = jnp.bitwise_and(order, WIDE - 1).astype(F32).astype(BF)
    rows = lax.broadcasted_iota(jnp.int32, (WIDE, order.shape[1]), 0).astype(F32).astype(BF)
    return jnp.where(rows == lane, jnp.ones((), BF), jnp.zeros((), BF))


def permuted(x, order, width):
    stacked = jnp.concatenate([x[:, h * WIDE : (h + 1) * WIDE] for h in range(BLOCKS)], axis=0)
    rows = x.shape[0]
    for start in range(0, order.shape[1], width):
        piece = order[:, start : start + width]
        picked = mm(stacked, low_onehot(piece))
        block = jnp.right_shift(piece, 8)
        total = jnp.zeros((rows, width), F32)
        for h in range(BLOCKS):
            total = total + jnp.where(block == h, picked[h * rows : (h + 1) * rows], 0.0)
        yield start, total.astype(BF)


def pack_message(x):
    return jnp.concatenate([x[:8], x[8:]], axis=1)


def fetch(sources, buffers, sems):
    copies = [
        pltpu.make_async_copy(source, buffer, sems.at[i])
        for i, (source, buffer) in enumerate(zip(sources, buffers, strict=True))
    ]
    for copy in copies:
        copy.start()
    return copies


def along_z(device):
    return jnp.bitwise_and(jnp.right_shift(device, 1), NLOW - 1)


def weights_first(device):
    return jnp.logical_and(along_z(device) < WEIGHTS_FIRST, device != 0)


def up_kernel(
    order_hbm, rhs_hbm, basis_hbm, transfer_hbm, top_transfer_hbm, top_coupling_hbm,
    sorted_ref, coef_ref, message_ref, low_hbm, high_hbm,
    order_ref, rhs_ref, basis_ref, transfer_ref, top_transfer_ref, top_coupling_ref, low_ref, high_ref, sems
):
    device = lax.axis_index("leaf")
    copies = fetch(
        (order_hbm, rhs_hbm, basis_hbm, transfer_hbm),
        (order_ref, rhs_ref, basis_ref, transfer_ref),
        sems,
    )
    copies[0].wait()
    copies[1].wait()
    x = rhs_ref[...].astype(BF)
    order = order_ref[...]
    block = jnp.right_shift(order, 8)
    places = low_onehot(order)
    copies[2].wait()
    copies[3].wait()
    stacked = jnp.concatenate([x[:, h * WIDE : (h + 1) * WIDE] for h in range(BLOCKS)], axis=0)
    picked = mm(stacked, places)
    total = jnp.where(block == 0, picked[:COLS], 0.0)
    for h in range(1, BLOCKS):
        total = total + jnp.where(block == h, picked[h * COLS : (h + 1) * COLS], 0.0)
    total = total.astype(BF)
    sorted_ref[...] = total
    coefs = []
    for n in range(LEAVES):
        coef = mm_nt(total[:, n * LEAF : (n + 1) * LEAF], basis_ref[n])
        coefs.append(coef)
        coef_ref[n] = coef
    hi, lo = halves(jnp.concatenate(coefs, axis=1))
    root = mm(jnp.concatenate([hi, lo], axis=0), transfer_ref[...].reshape(LEAVES * RANK, RANK))
    message = pack_message(root[:COLS] + root[COLS:])
    message_ref[...] = jnp.broadcast_to(message[None], message_ref.shape)

    @pl.when(weights_first(device))
    def _():
        for copy in fetch(
            (top_transfer_hbm, top_coupling_hbm), (top_transfer_ref, top_coupling_ref), sems
        ):
            copy.wait()
        form_weights(device, top_transfer_ref, top_coupling_ref, low_ref, high_ref)
        for copy in fetch((low_ref, high_ref), (low_hbm, high_hbm), sems):
            copy.wait()


def points_kernel(coords_hbm, order_hbm, sorted_ref, near_ref, across_ref, points_ref, coords_ref, order_ref, sems):
    copies = fetch((coords_hbm, order_hbm), (coords_ref, order_ref), sems)
    for copy in copies:
        copy.wait()
    x = jnp.concatenate([coords_ref[...], jnp.zeros((13, PTS), BF)], axis=0)
    for start, piece in permuted(x, order_ref[...], 2 * LEAF):
        points_ref[:, start : start + 2 * LEAF] = piece
    head = jnp.concatenate([sorted_ref[:, 0:LEAF], points_ref[:, 0:LEAF]], axis=0)
    tail = jnp.concatenate([sorted_ref[:, PTS - LEAF :], points_ref[:, PTS - LEAF :]], axis=0)
    even = jnp.bitwise_and(lax.axis_index("leaf"), 1) == 0

    @pl.when(even)
    def _():
        near_ref[...] = tail
        across_ref[...] = head

    @pl.when(jnp.logical_not(even))
    def _():
        near_ref[...] = head
        across_ref[...] = tail


def point_features(points):
    p = points.astype(F32)
    x, y, z = p[0:1], p[1:2], p[2:3]
    square = x * x + y * y + z * z
    s0 = square.astype(BF).astype(F32)
    rest = square - s0
    s1 = rest.astype(BF).astype(F32)
    s2 = rest - s1
    one = jnp.ones_like(square)
    zero = jnp.zeros((7, points.shape[1]), F32)
    source = jnp.concatenate([x, y, z, one, one, one, s0, s1, s2, zero], axis=0)
    target = jnp.concatenate(
        [-2.0 * x, -2.0 * y, -2.0 * z, s0, s1, s2, one, one, one, zero], axis=0
    )
    return source, target


def local_kernel(
    near_ref, far_ref, after_ref, coef_ref, coupling_ref, basis_ref, sorted_ref, points_ref, inner_ref, across_ref, out_ref,
    by_pair, spread, far, rhs, source, target, near
):
    del after_ref
    for first in range(0, RANK // 2, 8):
        turned = []
        for a in range(first, first + 8):
            two = jnp.concatenate([coupling_ref[a], coupling_ref[a + RANK // 2]], axis=0)
            turned.append(two.astype(F32).T)
        for j in range(0, LEAF, 8):
            block = jnp.stack([t[j : j + 8] for t in turned])
            by_pair[j : j + 8, first : first + 8, :] = jnp.swapaxes(block, 0, 1)
    zero = jnp.zeros((2 * COLS, RANK), BF)
    for n in range(LEAVES):
        hi, lo = halves(coef_ref[n])
        both = jnp.concatenate([hi, lo], axis=0)
        spread[n] = jnp.concatenate(
            [jnp.concatenate([both, zero], axis=1), jnp.concatenate([zero, both], axis=1)], axis=0
        )
    far[...] = jnp.zeros_like(far)
    near[...] = jnp.zeros_like(near)

    even = jnp.bitwise_and(lax.axis_index("leaf"), 1) == 0
    inner, across = inner_ref[...].astype(F32), across_ref[...].astype(F32)
    left = jnp.where(even, across, inner).astype(BF)
    right = jnp.where(even, inner, across).astype(BF)
    columns = jnp.concatenate([left[:COLS], sorted_ref[...], right[:COLS]], axis=1)
    points = jnp.concatenate([left[COLS:], points_ref[...], right[COLS:]], axis=1)
    of_source, of_target = point_features(points)
    of_target = of_target.astype(BF)
    for n in range(LEAVES + 2):
        here = slice(n * LEAF, (n + 1) * LEAF)
        rhs[n] = columns[:, here]
        source[n] = of_source[:, here].T.astype(BF)
        target[n] = of_target[:, here]

    def far_pair(j):
        to, of = far_ref[0, j], far_ref[1, j]
        rows = by_pair[j].astype(BF)
        far[to] += mm_nt(rows, spread[of])

    def near_pair(j):
        to, of = near_ref[0, j], near_ref[1, j]
        squared = jnp.maximum(mm(source[of], target[to + 1]) * (3.0 * LOG2E * LOG2E), 1e-30)
        scaled = squared * lax.rsqrt(squared)
        values = ((0.125 + (0.125 / LOG2E) * scaled) * jnp.exp2(-scaled)).astype(BF)
        near[to] += mm(rhs[of], values)

    for j in range(8 * LEAVES):
        far_pair(j)
    for j in range(3 * LEAVES):
        near_pair(j)
    for n in range(LEAVES):
        x = far[n].T
        field = jnp.concatenate(
            [x[:COLS] + x[COLS : 2 * COLS], x[2 * COLS : 3 * COLS] + x[3 * COLS :]], axis=1
        )
        hi, lo = halves(field)
        both = mm(jnp.concatenate([hi, lo], axis=0), basis_ref[n])
        out_ref[:, n * LEAF : (n + 1) * LEAF] = near[n] + (both[:COLS] + both[COLS:])


def times(a, b):
    hi, lo = halves(a)
    both = mm(jnp.concatenate([hi, lo], axis=0), b)
    return both[: a.shape[0]] + both[a.shape[0] :]


def weights_kernel(transfer_ref, coupling_ref, low_ref, high_ref):
    device = lax.axis_index("leaf")

    @pl.when(jnp.logical_not(weights_first(device)))
    def _():
        form_weights(device, transfer_ref, coupling_ref, low_ref, high_ref)


def form_weights(device, transfer_ref, coupling_ref, low_ref, high_ref):
    core = jnp.bitwise_and(device, 1)
    low = along_z(device)
    high = jnp.right_shift(device, LOW + 1)
    mine, other = transfer_ref[0, core], transfer_ref[0, 1 - core]

    hi, lo = halves(coupling_ref[0, 1 - core].astype(F32).T)
    zero = jnp.zeros((RANK, RANK), BF)
    low_ref[pl.ds(low, 1), :, 2 * RANK :] = jnp.concatenate([zero, hi, zero, lo], axis=1)[None]

    senders = mine.astype(F32)
    path = jnp.concatenate([mine, other], axis=0).astype(F32)
    for level in range(1, LOW + 1):
        h = level - 1
        node = jnp.right_shift(low, h)
        side = jnp.bitwise_and(node, 1)
        at = jnp.left_shift(jnp.bitwise_xor(node, 1), h)
        end = times(path, coupling_ref[level, side])
        hi, lo = halves(wide_nt(senders, end))
        low_ref[pl.ds(at, 1 << h), :, 2 * RANK :] = jnp.concatenate([hi, lo], axis=1).reshape(
            1 << h, RANK, 4 * RANK
        )
        path = times(path, transfer_ref[level, side])
        senders = jnp.concatenate(
            [times(senders, transfer_ref[level, 0]), times(senders, transfer_ref[level, 1])], axis=0
        )
    hi, lo = halves(senders)
    low_ref[:, :, : 2 * RANK] = jnp.concatenate([hi, lo], axis=1).reshape(NLOW, RANK, 2 * RANK)

    path = path[:RANK]
    high_ref[pl.ds(high, 1)] = jnp.zeros((1, RANK, 2 * RANK), BF)
    for h in range(HIGHS):
        level = LOW + 1 + h
        node = jnp.right_shift(high, h)
        side = jnp.bitwise_and(node, 1)
        at = jnp.left_shift(jnp.bitwise_xor(node, 1), h)
        end = times(path, coupling_ref[level, side])
        hi, lo = halves(end.T if h == 0 else wide_nt(senders, end))
        high_ref[pl.ds(at, 1 << h)] = jnp.concatenate([hi, lo], axis=1).reshape(
            1 << h, RANK, 2 * RANK
        )
        if h == HIGHS - 1:
            break
        path = times(path, transfer_ref[level, side])
        if h == 0:
            senders = transfer_ref[level].reshape(2 * RANK, RANK).astype(F32)
        else:
            senders = jnp.concatenate(
                [times(senders, transfer_ref[level, 0]), times(senders, transfer_ref[level, 1])], axis=0
            )


def unpacked(messages):
    x = jnp.concatenate([m[:, :RANK] for m in messages], axis=1)
    y = jnp.concatenate([m[:, RANK:] for m in messages], axis=1)
    hi, lo = halves(jnp.concatenate([x, y], axis=0))
    return jnp.concatenate([hi, lo], axis=0)


def middle_kernel(received_ref, early_ref, late_ref, message_ref, field_ref, result):
    device = lax.axis_index("leaf")
    received = unpacked([received_ref[(z - LEADER) % NLOW] for z in range(NLOW)])
    first = weights_first(device)

    @pl.when(first)
    def _():
        result[...] = mm(received, early_ref[...].reshape(NLOW * RANK, 6 * RANK))

    @pl.when(jnp.logical_not(first))
    def _():
        result[...] = mm(received, late_ref[...].reshape(NLOW * RANK, 6 * RANK))

    total = result[:COLS] + result[COLS:]
    node = total[:, :RANK] + total[:, RANK : 2 * RANK]
    fields = total[:, 2 * RANK : 4 * RANK] + total[:, 4 * RANK :]
    field_ref[...] = fields[:, :RANK]
    message_ref[...] = jnp.broadcast_to(pack_message(node)[None], message_ref.shape)
    high, core = jnp.right_shift(device, LOW + 1), jnp.bitwise_and(device, 1)
    at = jnp.bitwise_and(high - MIDDLE, NHIGH - 1)
    message_ref[at * 2 + 1 - core] = pack_message(fields[:, RANK:])


def down_kernel(
    received_ref, early_ref, late_ref, field_ref, partial_ref, transfer_hbm, basis_hbm, order_hbm, out_ref, transfer_ref, basis_ref, order_ref, sems
):
    copies = fetch(
        (transfer_hbm, basis_hbm, order_hbm), (transfer_ref, basis_ref, order_ref), sems
    )
    device = lax.axis_index("leaf")
    high, core = jnp.right_shift(device, LOW + 1), jnp.bitwise_and(device, 1)
    places = [(g - MIDDLE) % NHIGH for g in range(NHIGH)]
    total = mm(
        unpacked([received_ref[2 * g] + received_ref[2 * g + 1] for g in places]),
        jnp.where(weights_first(device), early_ref[...], late_ref[...]).reshape(NHIGH * RANK, 2 * RANK),
    )
    total = total[:COLS] + total[COLS:]
    sibling = received_ref[jnp.bitwise_and(high - MIDDLE, NHIGH - 1) * 2 + 1 - core]
    field = field_ref[...] + (total[:, :RANK] + total[:, RANK:])
    field = field + jnp.concatenate([sibling[:, :RANK], sibling[:, RANK:]], axis=0)
    hi, lo = halves(field)
    for copy in copies:
        copy.wait()
    fields = mm_nt(
        jnp.concatenate([hi, lo], axis=0), transfer_ref[...].reshape(LEAVES * RANK, RANK)
    )
    hi, lo = halves(fields[:COLS] + fields[COLS:])
    both = jnp.concatenate([hi, lo], axis=0)
    values = [mm(both[:, n * RANK : (n + 1) * RANK], basis_ref[n]) for n in range(LEAVES)]
    values = jnp.concatenate([v[:COLS] + v[COLS:] for v in values], axis=1) + partial_ref[...]
    hi, lo = halves(values)
    both = jnp.concatenate([hi, lo], axis=0)
    order = order_ref[...]
    block = jnp.right_shift(order, 8)
    masked = [both * jnp.where(block == h, 1.0, 0.0).astype(BF) for h in range(BLOCKS)]
    result = mm_nt(jnp.concatenate(masked, axis=0), low_onehot(order))
    for h in range(BLOCKS):
        at = h * 2 * COLS
        out_ref[:, h * WIDE : (h + 1) * WIDE] = result[at : at + COLS] + result[at + COLS : at + 2 * COLS]


def call(kernel, out, inputs, buffers=(), scratch=(), flops=0, transcendentals=0, vmem=16):
    shapes = [jax.ShapeDtypeStruct(o[0], o[1]) for o in out]
    scratches = [pltpu.VMEM(s, t) for s, t in buffers] + [pltpu.VMEM(s, t) for s, t in scratch]
    if buffers:
        scratches.append(pltpu.SemaphoreType.DMA((len(buffers),)))
    return pl.pallas_call(
        kernel,
        out_shape=shapes,
        in_specs=[space for space, _ in inputs],
        out_specs=[o[2] if len(o) > 2 else VMEM for o in out],
        scratch_shapes=scratches,
        compiler_params=pltpu.CompilerParams(vmem_limit_bytes=vmem << 20),
        cost_estimate=pl.CostEstimate(
            flops=flops, bytes_accessed=1 << 20, transcendentals=transcendentals
        ),
    )(*[array for _, array in inputs])


def per_device(
    right_sides,
    coordinates,
    tree_order,
    leaf_basis,
    far_pairs,
    far_coupling,
    near_pairs,
    leaf_transfer,
    top_transfer,
    top_coupling,
):
    count = lax.axis_size("leaf")
    order = tree_order.reshape(1, PTS)
    basis_like = (leaf_basis.shape, BF)
    transfer_like = (leaf_transfer.shape, BF)
    order_like = (order.shape, jnp.int32)
    low_like = ((NLOW, RANK, 6 * RANK), BF)
    high_like = ((NHIGH, RANK, 2 * RANK), BF)
    top_like = (top_transfer.shape, BF)
    sorted_rhs, coef, message, early_low, early_high = call(
        up_kernel,
        [
            ((COLS, PTS), BF),
            ((LEAVES, COLS, RANK), F32),
            ((NLOW, 8, 2 * RANK), F32),
            (*low_like, HBM),
            (*high_like, HBM),
        ],
        [
            (HBM, array)
            for array in (order, right_sides, leaf_basis, leaf_transfer, top_transfer, top_coupling)
        ],
        buffers=[order_like, (right_sides.shape, F32), basis_like, transfer_like]
        + [top_like, top_like, low_like, high_like],
        vmem=62,
        flops=1 << 28,
    )
    low_groups = [
        [(g * NLOW + (LEADER + z) % NLOW) * 2 + c for z in range(NLOW)]
        for g in range(NHIGH)
        for c in range(2)
    ]
    high_groups = [
        [((MIDDLE + g) % NHIGH * NLOW + z) * 2 + c for g in range(NHIGH) for c in range(2)]
        for z in range(NLOW)
    ]
    received = lax.all_to_all(message, "leaf", 0, 0, axis_index_groups=low_groups, tiled=True)

    inner, across, points = call(
        points_kernel,
        [((2 * COLS, LEAF), BF), ((2 * COLS, LEAF), BF), ((COLS, PTS), BF)],
        [(HBM, coordinates), (HBM, order), (VMEM, sorted_rhs)],
        buffers=[(coordinates.shape, BF), order_like],
        flops=1 << 28,
    )
    inner = lax.ppermute(inner, "leaf", [(i, i ^ 1) for i in range(count)])
    pairs = [(i, i + 1) for i in range(1, count - 1, 2)]
    across = lax.ppermute(across, "leaf", pairs + [(j, i) for i, j in pairs])
    late_low, late_high = call(
        weights_kernel,
        [low_like, high_like],
        [(VMEM, top_transfer), (VMEM, top_coupling)],
        flops=1 << 30,
    )
    message, field = call(
        middle_kernel,
        [((2 * NHIGH, 8, 2 * RANK), F32), ((COLS, RANK), F32)],
        [(VMEM, received), (VMEM, early_low), (VMEM, late_low)],
        scratch=[((2 * COLS, 6 * RANK), F32)],
        flops=1 << 27,
    )
    received = lax.all_to_all(message, "leaf", 0, 0, axis_index_groups=high_groups, tiled=True)
    coupling = far_coupling.transpose(1, 2, 0)
    (partial,) = call(
        local_kernel,
        [((COLS, PTS), F32)],
        [
            (SMEM, near_pairs),
            (SMEM, far_pairs),
            (ANY, field),
            (VMEM, coef),
            (VMEM, coupling),
            (VMEM, leaf_basis),
            (VMEM, sorted_rhs),
            (VMEM, points),
            (VMEM, inner),
            (VMEM, across),
        ],
        scratch=[
            ((LEAF, RANK // 2, 2 * RANK), F32),
            ((LEAVES, 4 * COLS, 2 * RANK), BF),
            ((LEAVES, RANK // 2, 4 * COLS), F32),
            ((LEAVES + 2, COLS, LEAF), BF),
            ((LEAVES + 2, LEAF, COLS), BF),
            ((LEAVES + 2, COLS, LEAF), BF),
            ((LEAVES, COLS, LEAF), F32),
        ],
        flops=1 << 32,
        transcendentals=1 << 21,
    )
    (product,) = call(
        down_kernel,
        [((COLS, PTS), F32)],
        [
            (VMEM, received),
            (VMEM, early_high),
            (VMEM, late_high),
            (VMEM, field),
            (VMEM, partial),
            (HBM, leaf_transfer),
            (HBM, leaf_basis),
            (HBM, order),
        ],
        buffers=[transfer_like, basis_like, order_like],
        flops=1 << 28,
    )
    return product


def solution(mesh):
    return jax.shard_map(
        per_device,
        mesh=mesh,
        in_specs=(
            P(None, "leaf"),
            P(None, "leaf"),
            P("leaf"),
            P("leaf", None, None),
            P(None, "leaf"),
            P("leaf", None, None),
            P(None, "leaf"),
            P("leaf", None, None),
            P(),
            P(),
        ),
        out_specs=P(None, "leaf"),
        check_vma=False,
    )
```

```python
import jax
import jax.numpy as jnp
from jax import lax
from jax.experimental import pallas as pl
from jax.experimental.pallas import tpu as pltpu
from jax.sharding import PartitionSpec as P

BF = jnp.bfloat16
F32 = jnp.float32
LEAF = 128
RANK = 64
COLS = 16
LEAVES = 16
WIDE = 256
BLOCKS = 8
PTS = LEAVES * LEAF
LOW = 4
HIGHS = 4
WEIGHTS_FIRST = 3
LEADER = 11
MIDDLE = 8
NLOW = 1 << LOW
NHIGH = 1 << HIGHS
LOG2E = 1.4426950408889634
VMEM = pl.BlockSpec(memory_space=pltpu.VMEM)
SMEM = pl.BlockSpec(memory_space=pltpu.SMEM)
ANY = pl.BlockSpec(memory_space=pl.ANY)
HBM = pl.BlockSpec(memory_space=pltpu.HBM)


def halves(x):
    hi = x.astype(BF)
    return hi, (x - hi.astype(F32)).astype(BF)


def mm(a, b):
    return jnp.dot(a, b, preferred_element_type=F32)


def mm_nt(a, b):
    return lax.dot_general(a, b, (((1,), (1,)), ((), ())), preferred_element_type=F32)


def wide(a, b):
    ah, al = halves(a)
    bh, bl = halves(b)
    return mm(ah, bh) + (mm(ah, bl) + mm(al, bh))


def wide_nt(a, b):
    ah, al = halves(a)
    bh, bl = halves(b)
    return mm_nt(ah, bh) + (mm_nt(ah, bl) + mm_nt(al, bh))


def low_onehot(order):
    lane = jnp.bitwise_and(order, WIDE - 1).astype(F32).astype(BF)
    rows = lax.broadcasted_iota(jnp.int32, (WIDE, order.shape[1]), 0).astype(F32).astype(BF)
    return jnp.where(rows == lane, jnp.ones((), BF), jnp.zeros((), BF))


def permuted(x, order, width):
    stacked = jnp.concatenate([x[:, h * WIDE : (h + 1) * WIDE] for h in range(BLOCKS)], axis=0)
    rows = x.shape[0]
    for start in range(0, order.shape[1], width):
        piece = order[:, start : start + width]
        picked = mm(stacked, low_onehot(piece))
        block = jnp.right_shift(piece, 8)
        total = jnp.zeros((rows, width), F32)
        for h in range(BLOCKS):
            total = total + jnp.where(block == h, picked[h * rows : (h + 1) * rows], 0.0)
        yield start, total.astype(BF)


def pack_message(x):
    return jnp.concatenate([x[:8], x[8:]], axis=1)


def fetch(sources, buffers, sems):
    copies = [
        pltpu.make_async_copy(source, buffer, sems.at[i])
        for i, (source, buffer) in enumerate(zip(sources, buffers, strict=True))
    ]
    for copy in copies:
        copy.start()
    return copies


def along_z(device):
    return jnp.bitwise_and(jnp.right_shift(device, 1), NLOW - 1)


def weights_first(device):
    return jnp.logical_and(along_z(device) < WEIGHTS_FIRST, device != 0)


def up_kernel(
    order_hbm, rhs_hbm, basis_hbm, transfer_hbm, top_transfer_hbm, top_coupling_hbm,
    sorted_ref, message_ref, low_hbm, high_hbm,
    order_ref, rhs_ref, basis_ref, transfer_ref, top_transfer_ref, top_coupling_ref, low_ref, high_ref, sems
):
    device = lax.axis_index("leaf")
    copies = fetch(
        (order_hbm, rhs_hbm, basis_hbm, transfer_hbm),
        (order_ref, rhs_ref, basis_ref, transfer_ref),
        sems,
    )
    copies[0].wait()
    copies[1].wait()
    x = rhs_ref[...].astype(BF)
    order = order_ref[...]
    block = jnp.right_shift(order, 8)
    places = low_onehot(order)
    copies[2].wait()
    copies[3].wait()
    stacked = jnp.concatenate([x[:, h * WIDE : (h + 1) * WIDE] for h in range(BLOCKS)], axis=0)
    picked = mm(stacked, places)
    total = jnp.where(block == 0, picked[:COLS], 0.0)
    for h in range(1, BLOCKS):
        total = total + jnp.where(block == h, picked[h * COLS : (h + 1) * COLS], 0.0)
    total = total.astype(BF)
    sorted_ref[...] = total
    coefs = []
    for n in range(LEAVES):
        coef = mm_nt(total[:, n * LEAF : (n + 1) * LEAF], basis_ref[n])
        coefs.append(coef)
    hi, lo = halves(jnp.concatenate(coefs, axis=1))
    root = mm(jnp.concatenate([hi, lo], axis=0), transfer_ref[...].reshape(LEAVES * RANK, RANK))
    message = pack_message(root[:COLS] + root[COLS:])
    message_ref[...] = jnp.broadcast_to(message[None], message_ref.shape)

    @pl.when(weights_first(device))
    def _():
        for copy in fetch(
            (top_transfer_hbm, top_coupling_hbm), (top_transfer_ref, top_coupling_ref), sems
        ):
            copy.wait()
        form_weights(device, top_transfer_ref, top_coupling_ref, low_ref, high_ref)
        for copy in fetch((low_ref, high_ref), (low_hbm, high_hbm), sems):
            copy.wait()


def points_kernel(coords_hbm, order_hbm, sorted_ref, near_ref, across_ref, points_ref, coords_ref, order_ref, sems):
    copies = fetch((coords_hbm, order_hbm), (coords_ref, order_ref), sems)
    for copy in copies:
        copy.wait()
    x = jnp.concatenate([coords_ref[...], jnp.zeros((13, PTS), BF)], axis=0)
    for start, piece in permuted(x, order_ref[...], 2 * LEAF):
        points_ref[:, start : start + 2 * LEAF] = piece
    head = jnp.concatenate([sorted_ref[:, 0:LEAF], points_ref[:, 0:LEAF]], axis=0)
    tail = jnp.concatenate([sorted_ref[:, PTS - LEAF :], points_ref[:, PTS - LEAF :]], axis=0)
    even = jnp.bitwise_and(lax.axis_index("leaf"), 1) == 0

    @pl.when(even)
    def _():
        near_ref[...] = tail
        across_ref[...] = head

    @pl.when(jnp.logical_not(even))
    def _():
        near_ref[...] = head
        across_ref[...] = tail


def point_features(points):
    p = points.astype(F32)
    x, y, z = p[0:1], p[1:2], p[2:3]
    square = x * x + y * y + z * z
    s0 = square.astype(BF).astype(F32)
    rest = square - s0
    s1 = rest.astype(BF).astype(F32)
    s2 = rest - s1
    one = jnp.ones_like(square)
    zero = jnp.zeros((7, points.shape[1]), F32)
    source = jnp.concatenate([x, y, z, one, one, one, s0, s1, s2, zero], axis=0)
    target = jnp.concatenate(
        [-2.0 * x, -2.0 * y, -2.0 * z, s0, s1, s2, one, one, one, zero], axis=0
    )
    return source, target


def local_kernel(
    near_ref, far_ref, after_ref, coupling_ref, basis_ref, sorted_ref, points_ref, inner_ref, across_ref, out_ref,
    by_pair, spread, far, rhs, source, target, near
):
    del after_ref
    for first in range(0, RANK // 2, 8):
        turned = []
        for a in range(first, first + 8):
            two = jnp.concatenate([coupling_ref[a], coupling_ref[a + RANK // 2]], axis=0)
            turned.append(two.astype(F32).T)
        for j in range(0, LEAF, 8):
            block = jnp.stack([t[j : j + 8] for t in turned])
            by_pair[j : j + 8, first : first + 8, :] = jnp.swapaxes(block, 0, 1)
    zero = jnp.zeros((2 * COLS, RANK), BF)
    for n in range(LEAVES):
        hi, lo = halves(mm_nt(sorted_ref[:, n * LEAF : (n + 1) * LEAF], basis_ref[n]))
        both = jnp.concatenate([hi, lo], axis=0)
        spread[n] = jnp.concatenate(
            [jnp.concatenate([both, zero], axis=1), jnp.concatenate([zero, both], axis=1)], axis=0
        )
    far[...] = jnp.zeros_like(far)
    near[...] = jnp.zeros_like(near)

    even = jnp.bitwise_and(lax.axis_index("leaf"), 1) == 0
    inner, across = inner_ref[...].astype(F32), across_ref[...].astype(F32)
    left = jnp.where(even, across, inner).astype(BF)
    right = jnp.where(even, inner, across).astype(BF)
    columns = jnp.concatenate([left[:COLS], sorted_ref[...], right[:COLS]], axis=1)
    points = jnp.concatenate([left[COLS:], points_ref[...], right[COLS:]], axis=1)
    of_source, of_target = point_features(points)
    of_target = of_target.astype(BF)
    for n in range(LEAVES + 2):
        here = slice(n * LEAF, (n + 1) * LEAF)
        rhs[n] = columns[:, here]
        source[n] = of_source[:, here].T.astype(BF)
        target[n] = of_target[:, here]

    def far_pair(j):
        to, of = far_ref[0, j], far_ref[1, j]
        rows = by_pair[j].astype(BF)
        far[to] += mm_nt(rows, spread[of])

    def near_pair(j):
        to, of = near_ref[0, j], near_ref[1, j]
        squared = jnp.maximum(mm(source[of], target[to + 1]) * (3.0 * LOG2E * LOG2E), 1e-30)
        scaled = squared * lax.rsqrt(squared)
        values = ((0.125 + (0.125 / LOG2E) * scaled) * jnp.exp2(-scaled)).astype(BF)
        near[to] += mm(rhs[of], values)

    for j in range(8 * LEAVES):
        far_pair(j)
    for j in range(3 * LEAVES):
        near_pair(j)
    for n in range(LEAVES):
        x = far[n].T
        field = jnp.concatenate(
            [x[:COLS] + x[COLS : 2 * COLS], x[2 * COLS : 3 * COLS] + x[3 * COLS :]], axis=1
        )
        hi, lo = halves(field)
        both = mm(jnp.concatenate([hi, lo], axis=0), basis_ref[n])
        out_ref[:, n * LEAF : (n + 1) * LEAF] = near[n] + (both[:COLS] + both[COLS:])


def times(a, b):
    hi, lo = halves(a)
    both = mm(jnp.concatenate([hi, lo], axis=0), b)
    return both[: a.shape[0]] + both[a.shape[0] :]


def weights_kernel(transfer_ref, coupling_ref, low_ref, high_ref):
    device = lax.axis_index("leaf")

    @pl.when(jnp.logical_not(weights_first(device)))
    def _():
        form_weights(device, transfer_ref, coupling_ref, low_ref, high_ref)


def form_weights(device, transfer_ref, coupling_ref, low_ref, high_ref):
    core = jnp.bitwise_and(device, 1)
    low = along_z(device)
    high = jnp.right_shift(device, LOW + 1)
    mine, other = transfer_ref[0, core], transfer_ref[0, 1 - core]

    hi, lo = halves(coupling_ref[0, 1 - core].astype(F32).T)
    zero = jnp.zeros((RANK, RANK), BF)
    low_ref[pl.ds(low, 1), :, 2 * RANK :] = jnp.concatenate([zero, hi, zero, lo], axis=1)[None]

    senders = mine.astype(F32)
    path = jnp.concatenate([mine, other], axis=0).astype(F32)
    for level in range(1, LOW + 1):
        h = level - 1
        node = jnp.right_shift(low, h)
        side = jnp.bitwise_and(node, 1)
        at = jnp.left_shift(jnp.bitwise_xor(node, 1), h)
        end = times(path, coupling_ref[level, side])
        hi, lo = halves(wide_nt(senders, end))
        low_ref[pl.ds(at, 1 << h), :, 2 * RANK :] = jnp.concatenate([hi, lo], axis=1).reshape(
            1 << h, RANK, 4 * RANK
        )
        path = times(path, transfer_ref[level, side])
        senders = jnp.concatenate(
            [times(senders, transfer_ref[level, 0]), times(senders, transfer_ref[level, 1])], axis=0
        )
    hi, lo = halves(senders)
    low_ref[:, :, : 2 * RANK] = jnp.concatenate([hi, lo], axis=1).reshape(NLOW, RANK, 2 * RANK)

    path = path[:RANK]
    high_ref[pl.ds(high, 1)] = jnp.zeros((1, RANK, 2 * RANK), BF)
    for h in range(HIGHS):
        level = LOW + 1 + h
        node = jnp.right_shift(high, h)
        side = jnp.bitwise_and(node, 1)
        at = jnp.left_shift(jnp.bitwise_xor(node, 1), h)
        end = times(path, coupling_ref[level, side])
        hi, lo = halves(end.T if h == 0 else wide_nt(senders, end))
        high_ref[pl.ds(at, 1 << h)] = jnp.concatenate([hi, lo], axis=1).reshape(
            1 << h, RANK, 2 * RANK
        )
        if h == HIGHS - 1:
            break
        path = times(path, transfer_ref[level, side])
        if h == 0:
            senders = transfer_ref[level].reshape(2 * RANK, RANK).astype(F32)
        else:
            senders = jnp.concatenate(
                [times(senders, transfer_ref[level, 0]), times(senders, transfer_ref[level, 1])], axis=0
            )


def unpacked(messages):
    x = jnp.concatenate([m[:, :RANK] for m in messages], axis=1)
    y = jnp.concatenate([m[:, RANK:] for m in messages], axis=1)
    hi, lo = halves(jnp.concatenate([x, y], axis=0))
    return jnp.concatenate([hi, lo], axis=0)


def middle_kernel(received_ref, early_ref, late_ref, message_ref, field_ref, result):
    device = lax.axis_index("leaf")
    received = unpacked([received_ref[(z - LEADER) % NLOW] for z in range(NLOW)])
    first = weights_first(device)

    @pl.when(first)
    def _():
        result[...] = mm(received, early_ref[...].reshape(NLOW * RANK, 6 * RANK))

    @pl.when(jnp.logical_not(first))
    def _():
        result[...] = mm(received, late_ref[...].reshape(NLOW * RANK, 6 * RANK))

    total = result[:COLS] + result[COLS:]
    node = total[:, :RANK] + total[:, RANK : 2 * RANK]
    fields = total[:, 2 * RANK : 4 * RANK] + total[:, 4 * RANK :]
    field_ref[...] = fields[:, :RANK]
    message_ref[...] = jnp.broadcast_to(pack_message(node)[None], message_ref.shape)
    high, core = jnp.right_shift(device, LOW + 1), jnp.bitwise_and(device, 1)
    at = jnp.bitwise_and(high - MIDDLE, NHIGH - 1)
    message_ref[at * 2 + 1 - core] = pack_message(fields[:, RANK:])


def down_kernel(
    received_ref, early_ref, late_ref, field_ref, partial_ref, transfer_hbm, basis_hbm, order_hbm, out_ref, transfer_ref, basis_ref, order_ref, sems
):
    copies = fetch(
        (transfer_hbm, basis_hbm, order_hbm), (transfer_ref, basis_ref, order_ref), sems
    )
    device = lax.axis_index("leaf")
    high, core = jnp.right_shift(device, LOW + 1), jnp.bitwise_and(device, 1)
    places = [(g - MIDDLE) % NHIGH for g in range(NHIGH)]
    total = mm(
        unpacked([received_ref[2 * g] + received_ref[2 * g + 1] for g in places]),
        jnp.where(weights_first(device), early_ref[...], late_ref[...]).reshape(NHIGH * RANK, 2 * RANK),
    )
    total = total[:COLS] + total[COLS:]
    sibling = received_ref[jnp.bitwise_and(high - MIDDLE, NHIGH - 1) * 2 + 1 - core]
    field = field_ref[...] + (total[:, :RANK] + total[:, RANK:])
    field = field + jnp.concatenate([sibling[:, :RANK], sibling[:, RANK:]], axis=0)
    hi, lo = halves(field)
    for copy in copies:
        copy.wait()
    fields = mm_nt(
        jnp.concatenate([hi, lo], axis=0), transfer_ref[...].reshape(LEAVES * RANK, RANK)
    )
    hi, lo = halves(fields[:COLS] + fields[COLS:])
    both = jnp.concatenate([hi, lo], axis=0)
    values = [mm(both[:, n * RANK : (n + 1) * RANK], basis_ref[n]) for n in range(LEAVES)]
    values = jnp.concatenate([v[:COLS] + v[COLS:] for v in values], axis=1) + partial_ref[...]
    hi, lo = halves(values)
    both = jnp.concatenate([hi, lo], axis=0)
    order = order_ref[...]
    block = jnp.right_shift(order, 8)
    masked = [both * jnp.where(block == h, 1.0, 0.0).astype(BF) for h in range(BLOCKS)]
    result = mm_nt(jnp.concatenate(masked, axis=0), low_onehot(order))
    for h in range(BLOCKS):
        at = h * 2 * COLS
        out_ref[:, h * WIDE : (h + 1) * WIDE] = result[at : at + COLS] + result[at + COLS : at + 2 * COLS]


def call(kernel, out, inputs, buffers=(), scratch=(), flops=0, transcendentals=0, vmem=16):
    shapes = [jax.ShapeDtypeStruct(o[0], o[1]) for o in out]
    scratches = [pltpu.VMEM(s, t) for s, t in buffers] + [pltpu.VMEM(s, t) for s, t in scratch]
    if buffers:
        scratches.append(pltpu.SemaphoreType.DMA((len(buffers),)))
    return pl.pallas_call(
        kernel,
        out_shape=shapes,
        in_specs=[space for space, _ in inputs],
        out_specs=[o[2] if len(o) > 2 else VMEM for o in out],
        scratch_shapes=scratches,
        compiler_params=pltpu.CompilerParams(vmem_limit_bytes=vmem << 20),
        cost_estimate=pl.CostEstimate(
            flops=flops, bytes_accessed=1 << 20, transcendentals=transcendentals
        ),
    )(*[array for _, array in inputs])


def per_device(
    right_sides,
    coordinates,
    tree_order,
    leaf_basis,
    far_pairs,
    far_coupling,
    near_pairs,
    leaf_transfer,
    top_transfer,
    top_coupling,
):
    count = lax.axis_size("leaf")
    order = tree_order.reshape(1, PTS)
    basis_like = (leaf_basis.shape, BF)
    transfer_like = (leaf_transfer.shape, BF)
    order_like = (order.shape, jnp.int32)
    low_like = ((NLOW, RANK, 6 * RANK), BF)
    high_like = ((NHIGH, RANK, 2 * RANK), BF)
    top_like = (top_transfer.shape, BF)
    sorted_rhs, message, early_low, early_high = call(
        up_kernel,
        [
            ((COLS, PTS), BF),
            ((NLOW, 8, 2 * RANK), F32),
            (*low_like, HBM),
            (*high_like, HBM),
        ],
        [
            (HBM, array)
            for array in (order, right_sides, leaf_basis, leaf_transfer, top_transfer, top_coupling)
        ],
        buffers=[order_like, (right_sides.shape, F32), basis_like, transfer_like]
        + [top_like, top_like, low_like, high_like],
        vmem=62,
        flops=1 << 28,
    )
    low_groups = [
        [(g * NLOW + (LEADER + z) % NLOW) * 2 + c for z in range(NLOW)]
        for g in range(NHIGH)
        for c in range(2)
    ]
    high_groups = [
        [((MIDDLE + g) % NHIGH * NLOW + z) * 2 + c for g in range(NHIGH) for c in range(2)]
        for z in range(NLOW)
    ]
    received = lax.all_to_all(message, "leaf", 0, 0, axis_index_groups=low_groups, tiled=True)

    inner, across, points = call(
        points_kernel,
        [((2 * COLS, LEAF), BF), ((2 * COLS, LEAF), BF), ((COLS, PTS), BF)],
        [(HBM, coordinates), (HBM, order), (VMEM, sorted_rhs)],
        buffers=[(coordinates.shape, BF), order_like],
        flops=1 << 28,
    )
    inner = lax.ppermute(inner, "leaf", [(i, i ^ 1) for i in range(count)])
    pairs = [(i, i + 1) for i in range(1, count - 1, 2)]
    across = lax.ppermute(across, "leaf", pairs + [(j, i) for i, j in pairs])
    late_low, late_high = call(
        weights_kernel,
        [low_like, high_like],
        [(VMEM, top_transfer), (VMEM, top_coupling)],
        flops=1 << 30,
    )
    message, field = call(
        middle_kernel,
        [((2 * NHIGH, 8, 2 * RANK), F32), ((COLS, RANK), F32)],
        [(VMEM, received), (VMEM, early_low), (VMEM, late_low)],
        scratch=[((2 * COLS, 6 * RANK), F32)],
        flops=1 << 27,
    )
    received = lax.all_to_all(message, "leaf", 0, 0, axis_index_groups=high_groups, tiled=True)
    coupling = far_coupling.transpose(1, 2, 0)
    (partial,) = call(
        local_kernel,
        [((COLS, PTS), F32)],
        [
            (SMEM, near_pairs),
            (SMEM, far_pairs),
            (ANY, field),
            (VMEM, coupling),
            (VMEM, leaf_basis),
            (VMEM, sorted_rhs),
            (VMEM, points),
            (VMEM, inner),
            (VMEM, across),
        ],
        scratch=[
            ((LEAF, RANK // 2, 2 * RANK), F32),
            ((LEAVES, 4 * COLS, 2 * RANK), BF),
            ((LEAVES, RANK // 2, 4 * COLS), F32),
            ((LEAVES + 2, COLS, LEAF), BF),
            ((LEAVES + 2, LEAF, COLS), BF),
            ((LEAVES + 2, COLS, LEAF), BF),
            ((LEAVES, COLS, LEAF), F32),
        ],
        flops=1 << 32,
        transcendentals=1 << 21,
    )
    (product,) = call(
        down_kernel,
        [((COLS, PTS), F32)],
        [
            (VMEM, received),
            (VMEM, early_high),
            (VMEM, late_high),
            (VMEM, field),
            (VMEM, partial),
            (HBM, leaf_transfer),
            (HBM, leaf_basis),
            (HBM, order),
        ],
        buffers=[transfer_like, basis_like, order_like],
        flops=1 << 28,
    )
    return product


def solution(mesh):
    return jax.shard_map(
        per_device,
        mesh=mesh,
        in_specs=(
            P(None, "leaf"),
            P(None, "leaf"),
            P("leaf"),
            P("leaf", None, None),
            P(None, "leaf"),
            P("leaf", None, None),
            P(None, "leaf"),
            P("leaf", None, None),
            P(),
            P(),
        ),
        out_specs=P(None, "leaf"),
        check_vma=False,
    )
```

```python
import jax
import jax.numpy as jnp
from jax import lax
from jax.experimental import pallas as pl
from jax.experimental.pallas import tpu as pltpu
from jax.sharding import PartitionSpec as P

BF = jnp.bfloat16
F32 = jnp.float32
LEAF = 128
RANK = 64
COLS = 16
LEAVES = 16
WIDE = 256
BLOCKS = 8
PTS = LEAVES * LEAF
LOW = 4
HIGHS = 4
WEIGHTS_FIRST = 3
LEADER = 11
MIDDLE = 8
NLOW = 1 << LOW
NHIGH = 1 << HIGHS
LOG2E = 1.4426950408889634
VMEM = pl.BlockSpec(memory_space=pltpu.VMEM)
SMEM = pl.BlockSpec(memory_space=pltpu.SMEM)
ANY = pl.BlockSpec(memory_space=pl.ANY)
HBM = pl.BlockSpec(memory_space=pltpu.HBM)


def halves(x):
    hi = x.astype(BF)
    return hi, (x - hi.astype(F32)).astype(BF)


def mm(a, b):
    return jnp.dot(a, b, preferred_element_type=F32)


def mm_nt(a, b):
    return lax.dot_general(a, b, (((1,), (1,)), ((), ())), preferred_element_type=F32)


def wide(a, b):
    ah, al = halves(a)
    bh, bl = halves(b)
    return mm(ah, bh) + (mm(ah, bl) + mm(al, bh))


def wide_nt(a, b):
    ah, al = halves(a)
    bh, bl = halves(b)
    return mm_nt(ah, bh) + (mm_nt(ah, bl) + mm_nt(al, bh))


def low_onehot(order):
    lane = jnp.bitwise_and(order, WIDE - 1).astype(F32).astype(BF)
    rows = lax.broadcasted_iota(jnp.int32, (WIDE, order.shape[1]), 0).astype(F32).astype(BF)
    return jnp.where(rows == lane, jnp.ones((), BF), jnp.zeros((), BF))


def permuted(x, order, width):
    stacked = jnp.concatenate([x[:, h * WIDE : (h + 1) * WIDE] for h in range(BLOCKS)], axis=0)
    rows = x.shape[0]
    for start in range(0, order.shape[1], width):
        piece = order[:, start : start + width]
        picked = mm(stacked, low_onehot(piece))
        block = jnp.right_shift(piece, 8)
        total = jnp.zeros((rows, width), F32)
        for h in range(BLOCKS):
            total = total + jnp.where(block == h, picked[h * rows : (h + 1) * rows], 0.0)
        yield start, total.astype(BF)


def pack_message(x):
    return jnp.concatenate([x[:8], x[8:]], axis=1)


def fetch(sources, buffers, sems):
    copies = [
        pltpu.make_async_copy(source, buffer, sems.at[i])
        for i, (source, buffer) in enumerate(zip(sources, buffers, strict=True))
    ]
    for copy in copies:
        copy.start()
    return copies


def along_z(device):
    return jnp.bitwise_and(jnp.right_shift(device, 1), NLOW - 1)


def weights_first(device):
    return jnp.logical_and(along_z(device) < WEIGHTS_FIRST, device != 0)


def up_kernel(
    order_hbm, rhs_hbm, basis_hbm, transfer_hbm, top_transfer_hbm, top_coupling_hbm,
    sorted_ref, message_ref, low_hbm, high_hbm,
    order_ref, rhs_ref, basis_ref, transfer_ref, top_transfer_ref, top_coupling_ref, low_ref, high_ref, sems
):
    device = lax.axis_index("leaf")
    copies = fetch(
        (order_hbm, rhs_hbm, basis_hbm, transfer_hbm),
        (order_ref, rhs_ref, basis_ref, transfer_ref),
        sems,
    )
    copies[0].wait()
    order = order_ref[...]
    block = jnp.right_shift(order, 8)
    places = low_onehot(order)
    copies[1].wait()
    x = rhs_ref[...].astype(BF)
    copies[2].wait()
    copies[3].wait()
    stacked = jnp.concatenate([x[:, h * WIDE : (h + 1) * WIDE] for h in range(BLOCKS)], axis=0)
    picked = mm(stacked, places)
    total = jnp.where(block == 0, picked[:COLS], 0.0)
    for h in range(1, BLOCKS):
        total = total + jnp.where(block == h, picked[h * COLS : (h + 1) * COLS], 0.0)
    total = total.astype(BF)
    sorted_ref[...] = total
    coefs = []
    for n in range(LEAVES):
        coef = mm_nt(total[:, n * LEAF : (n + 1) * LEAF], basis_ref[n])
        coefs.append(coef)
    hi, lo = halves(jnp.concatenate(coefs, axis=1))
    root = mm(jnp.concatenate([hi, lo], axis=0), transfer_ref[...].reshape(LEAVES * RANK, RANK))
    message = pack_message(root[:COLS] + root[COLS:])
    message_ref[...] = jnp.broadcast_to(message[None], message_ref.shape)

    @pl.when(weights_first(device))
    def _():
        for copy in fetch(
            (top_transfer_hbm, top_coupling_hbm), (top_transfer_ref, top_coupling_ref), sems
        ):
            copy.wait()
        form_weights(device, top_transfer_ref, top_coupling_ref, low_ref, high_ref)
        for copy in fetch((low_ref, high_ref), (low_hbm, high_hbm), sems):
            copy.wait()


def points_kernel(coords_hbm, order_hbm, sorted_ref, near_ref, across_ref, points_ref, coords_ref, order_ref, sems):
    copies = fetch((coords_hbm, order_hbm), (coords_ref, order_ref), sems)
    for copy in copies:
        copy.wait()
    x = jnp.concatenate([coords_ref[...], jnp.zeros((13, PTS), BF)], axis=0)
    for start, piece in permuted(x, order_ref[...], 2 * LEAF):
        points_ref[:, start : start + 2 * LEAF] = piece
    head = jnp.concatenate([sorted_ref[:, 0:LEAF], points_ref[:, 0:LEAF]], axis=0)
    tail = jnp.concatenate([sorted_ref[:, PTS - LEAF :], points_ref[:, PTS - LEAF :]], axis=0)
    even = jnp.bitwise_and(lax.axis_index("leaf"), 1) == 0

    @pl.when(even)
    def _():
        near_ref[...] = tail
        across_ref[...] = head

    @pl.when(jnp.logical_not(even))
    def _():
        near_ref[...] = head
        across_ref[...] = tail


def point_features(points):
    p = points.astype(F32)
    x, y, z = p[0:1], p[1:2], p[2:3]
    square = x * x + y * y + z * z
    s0 = square.astype(BF).astype(F32)
    rest = square - s0
    s1 = rest.astype(BF).astype(F32)
    s2 = rest - s1
    one = jnp.ones_like(square)
    zero = jnp.zeros((7, points.shape[1]), F32)
    source = jnp.concatenate([x, y, z, one, one, one, s0, s1, s2, zero], axis=0)
    target = jnp.concatenate(
        [-2.0 * x, -2.0 * y, -2.0 * z, s0, s1, s2, one, one, one, zero], axis=0
    )
    return source, target


def local_kernel(
    near_ref, far_ref, after_ref, coupling_ref, basis_ref, sorted_ref, points_ref, inner_ref, across_ref, out_ref,
    by_pair, spread, far, rhs, source, target, near
):
    del after_ref
    for first in range(0, RANK // 2, 8):
        turned = []
        for a in range(first, first + 8):
            two = jnp.concatenate([coupling_ref[a], coupling_ref[a + RANK // 2]], axis=0)
            turned.append(two.astype(F32).T)
        for j in range(0, LEAF, 8):
            block = jnp.stack([t[j : j + 8] for t in turned])
            by_pair[j : j + 8, first : first + 8, :] = jnp.swapaxes(block, 0, 1)
    zero = jnp.zeros((2 * COLS, RANK), BF)
    for n in range(LEAVES):
        hi, lo = halves(mm_nt(sorted_ref[:, n * LEAF : (n + 1) * LEAF], basis_ref[n]))
        both = jnp.concatenate([hi, lo], axis=0)
        spread[n] = jnp.concatenate(
            [jnp.concatenate([both, zero], axis=1), jnp.concatenate([zero, both], axis=1)], axis=0
        )
    far[...] = jnp.zeros_like(far)
    near[...] = jnp.zeros_like(near)

    even = jnp.bitwise_and(lax.axis_index("leaf"), 1) == 0
    inner, across = inner_ref[...].astype(F32), across_ref[...].astype(F32)
    left = jnp.where(even, across, inner).astype(BF)
    right = jnp.where(even, inner, across).astype(BF)
    columns = jnp.concatenate([left[:COLS], sorted_ref[...], right[:COLS]], axis=1)
    points = jnp.concatenate([left[COLS:], points_ref[...], right[COLS:]], axis=1)
    of_source, of_target = point_features(points)
    of_target = of_target.astype(BF)
    for n in range(LEAVES + 2):
        here = slice(n * LEAF, (n + 1) * LEAF)
        rhs[n] = columns[:, here]
        source[n] = of_source[:, here].T.astype(BF)
        target[n] = of_target[:, here]

    def far_pair(j):
        to, of = far_ref[0, j], far_ref[1, j]
        rows = by_pair[j].astype(BF)
        far[to] += mm_nt(rows, spread[of])

    def near_pair(j):
        to, of = near_ref[0, j], near_ref[1, j]
        squared = jnp.maximum(mm(source[of], target[to + 1]) * (3.0 * LOG2E * LOG2E), 1e-30)
        scaled = squared * lax.rsqrt(squared)
        values = ((0.125 + (0.125 / LOG2E) * scaled) * jnp.exp2(-scaled)).astype(BF)
        near[to] += mm(rhs[of], values)

    for j in range(8 * LEAVES):
        far_pair(j)
    for j in range(3 * LEAVES):
        near_pair(j)
    for n in range(LEAVES):
        x = far[n].T
        field = jnp.concatenate(
            [x[:COLS] + x[COLS : 2 * COLS], x[2 * COLS : 3 * COLS] + x[3 * COLS :]], axis=1
        )
        hi, lo = halves(field)
        both = mm(jnp.concatenate([hi, lo], axis=0), basis_ref[n])
        out_ref[:, n * LEAF : (n + 1) * LEAF] = near[n] + (both[:COLS] + both[COLS:])


def times(a, b):
    hi, lo = halves(a)
    both = mm(jnp.concatenate([hi, lo], axis=0), b)
    return both[: a.shape[0]] + both[a.shape[0] :]


def weights_kernel(transfer_ref, coupling_ref, low_ref, high_ref):
    device = lax.axis_index("leaf")

    @pl.when(jnp.logical_not(weights_first(device)))
    def _():
        form_weights(device, transfer_ref, coupling_ref, low_ref, high_ref)


def form_weights(device, transfer_ref, coupling_ref, low_ref, high_ref):
    core = jnp.bitwise_and(device, 1)
    low = along_z(device)
    high = jnp.right_shift(device, LOW + 1)
    mine, other = transfer_ref[0, core], transfer_ref[0, 1 - core]

    hi, lo = halves(coupling_ref[0, 1 - core].astype(F32).T)
    zero = jnp.zeros((RANK, RANK), BF)
    low_ref[pl.ds(low, 1), :, 2 * RANK :] = jnp.concatenate([zero, hi, zero, lo], axis=1)[None]

    senders = mine.astype(F32)
    path = jnp.concatenate([mine, other], axis=0).astype(F32)
    for level in range(1, LOW + 1):
        h = level - 1
        node = jnp.right_shift(low, h)
        side = jnp.bitwise_and(node, 1)
        at = jnp.left_shift(jnp.bitwise_xor(node, 1), h)
        end = times(path, coupling_ref[level, side])
        hi, lo = halves(wide_nt(senders, end))
        low_ref[pl.ds(at, 1 << h), :, 2 * RANK :] = jnp.concatenate([hi, lo], axis=1).reshape(
            1 << h, RANK, 4 * RANK
        )
        path = times(path, transfer_ref[level, side])
        senders = jnp.concatenate(
            [times(senders, transfer_ref[level, 0]), times(senders, transfer_ref[level, 1])], axis=0
        )
    hi, lo = halves(senders)
    low_ref[:, :, : 2 * RANK] = jnp.concatenate([hi, lo], axis=1).reshape(NLOW, RANK, 2 * RANK)

    path = path[:RANK]
    high_ref[pl.ds(high, 1)] = jnp.zeros((1, RANK, 2 * RANK), BF)
    for h in range(HIGHS):
        level = LOW + 1 + h
        node = jnp.right_shift(high, h)
        side = jnp.bitwise_and(node, 1)
        at = jnp.left_shift(jnp.bitwise_xor(node, 1), h)
        end = times(path, coupling_ref[level, side])
        hi, lo = halves(end.T if h == 0 else wide_nt(senders, end))
        high_ref[pl.ds(at, 1 << h)] = jnp.concatenate([hi, lo], axis=1).reshape(
            1 << h, RANK, 2 * RANK
        )
        if h == HIGHS - 1:
            break
        path = times(path, transfer_ref[level, side])
        if h == 0:
            senders = transfer_ref[level].reshape(2 * RANK, RANK).astype(F32)
        else:
            senders = jnp.concatenate(
                [times(senders, transfer_ref[level, 0]), times(senders, transfer_ref[level, 1])], axis=0
            )


def unpacked(messages):
    x = jnp.concatenate([m[:, :RANK] for m in messages], axis=1)
    y = jnp.concatenate([m[:, RANK:] for m in messages], axis=1)
    hi, lo = halves(jnp.concatenate([x, y], axis=0))
    return jnp.concatenate([hi, lo], axis=0)


def middle_kernel(received_ref, early_ref, late_ref, message_ref, field_ref, result):
    device = lax.axis_index("leaf")
    received = unpacked([received_ref[(z - LEADER) % NLOW] for z in range(NLOW)])
    first = weights_first(device)

    @pl.when(first)
    def _():
        result[...] = mm(received, early_ref[...].reshape(NLOW * RANK, 6 * RANK))

    @pl.when(jnp.logical_not(first))
    def _():
        result[...] = mm(received, late_ref[...].reshape(NLOW * RANK, 6 * RANK))

    total = result[:COLS] + result[COLS:]
    node = total[:, :RANK] + total[:, RANK : 2 * RANK]
    fields = total[:, 2 * RANK : 4 * RANK] + total[:, 4 * RANK :]
    field_ref[...] = fields[:, :RANK]
    message_ref[...] = jnp.broadcast_to(pack_message(node)[None], message_ref.shape)
    high, core = jnp.right_shift(device, LOW + 1), jnp.bitwise_and(device, 1)
    at = jnp.bitwise_and(high - MIDDLE, NHIGH - 1)
    message_ref[at * 2 + 1 - core] = pack_message(fields[:, RANK:])


def down_kernel(
    received_ref, early_ref, late_ref, field_ref, partial_ref, transfer_hbm, basis_hbm, order_hbm, out_ref, transfer_ref, basis_ref, order_ref, sems
):
    copies = fetch(
        (transfer_hbm, basis_hbm, order_hbm), (transfer_ref, basis_ref, order_ref), sems
    )
    device = lax.axis_index("leaf")
    high, core = jnp.right_shift(device, LOW + 1), jnp.bitwise_and(device, 1)
    places = [(g - MIDDLE) % NHIGH for g in range(NHIGH)]
    total = mm(
        unpacked([received_ref[2 * g] + received_ref[2 * g + 1] for g in places]),
        jnp.where(weights_first(device), early_ref[...], late_ref[...]).reshape(NHIGH * RANK, 2 * RANK),
    )
    total = total[:COLS] + total[COLS:]
    sibling = received_ref[jnp.bitwise_and(high - MIDDLE, NHIGH - 1) * 2 + 1 - core]
    field = field_ref[...] + (total[:, :RANK] + total[:, RANK:])
    field = field + jnp.concatenate([sibling[:, :RANK], sibling[:, RANK:]], axis=0)
    hi, lo = halves(field)
    for copy in copies:
        copy.wait()
    fields = mm_nt(
        jnp.concatenate([hi, lo], axis=0), transfer_ref[...].reshape(LEAVES * RANK, RANK)
    )
    hi, lo = halves(fields[:COLS] + fields[COLS:])
    both = jnp.concatenate([hi, lo], axis=0)
    values = [mm(both[:, n * RANK : (n + 1) * RANK], basis_ref[n]) for n in range(LEAVES)]
    values = jnp.concatenate([v[:COLS] + v[COLS:] for v in values], axis=1) + partial_ref[...]
    hi, lo = halves(values)
    both = jnp.concatenate([hi, lo], axis=0)
    order = order_ref[...]
    block = jnp.right_shift(order, 8)
    masked = [both * jnp.where(block == h, 1.0, 0.0).astype(BF) for h in range(BLOCKS)]
    result = mm_nt(jnp.concatenate(masked, axis=0), low_onehot(order))
    for h in range(BLOCKS):
        at = h * 2 * COLS
        out_ref[:, h * WIDE : (h + 1) * WIDE] = result[at : at + COLS] + result[at + COLS : at + 2 * COLS]


def call(kernel, out, inputs, buffers=(), scratch=(), flops=0, transcendentals=0, vmem=16):
    shapes = [jax.ShapeDtypeStruct(o[0], o[1]) for o in out]
    scratches = [pltpu.VMEM(s, t) for s, t in buffers] + [pltpu.VMEM(s, t) for s, t in scratch]
    if buffers:
        scratches.append(pltpu.SemaphoreType.DMA((len(buffers),)))
    return pl.pallas_call(
        kernel,
        out_shape=shapes,
        in_specs=[space for space, _ in inputs],
        out_specs=[o[2] if len(o) > 2 else VMEM for o in out],
        scratch_shapes=scratches,
        compiler_params=pltpu.CompilerParams(vmem_limit_bytes=vmem << 20),
        cost_estimate=pl.CostEstimate(
            flops=flops, bytes_accessed=1 << 20, transcendentals=transcendentals
        ),
    )(*[array for _, array in inputs])


def per_device(
    right_sides,
    coordinates,
    tree_order,
    leaf_basis,
    far_pairs,
    far_coupling,
    near_pairs,
    leaf_transfer,
    top_transfer,
    top_coupling,
):
    count = lax.axis_size("leaf")
    order = tree_order.reshape(1, PTS)
    basis_like = (leaf_basis.shape, BF)
    transfer_like = (leaf_transfer.shape, BF)
    order_like = (order.shape, jnp.int32)
    low_like = ((NLOW, RANK, 6 * RANK), BF)
    high_like = ((NHIGH, RANK, 2 * RANK), BF)
    top_like = (top_transfer.shape, BF)
    sorted_rhs, message, early_low, early_high = call(
        up_kernel,
        [
            ((COLS, PTS), BF),
            ((NLOW, 8, 2 * RANK), F32),
            (*low_like, HBM),
            (*high_like, HBM),
        ],
        [
            (HBM, array)
            for array in (order, right_sides, leaf_basis, leaf_transfer, top_transfer, top_coupling)
        ],
        buffers=[order_like, (right_sides.shape, F32), basis_like, transfer_like]
        + [top_like, top_like, low_like, high_like],
        vmem=62,
        flops=1 << 28,
    )
    low_groups = [
        [(g * NLOW + (LEADER + z) % NLOW) * 2 + c for z in range(NLOW)]
        for g in range(NHIGH)
        for c in range(2)
    ]
    high_groups = [
        [((MIDDLE + g) % NHIGH * NLOW + z) * 2 + c for g in range(NHIGH) for c in range(2)]
        for z in range(NLOW)
    ]
    received = lax.all_to_all(message, "leaf", 0, 0, axis_index_groups=low_groups, tiled=True)

    inner, across, points = call(
        points_kernel,
        [((2 * COLS, LEAF), BF), ((2 * COLS, LEAF), BF), ((COLS, PTS), BF)],
        [(HBM, coordinates), (HBM, order), (VMEM, sorted_rhs)],
        buffers=[(coordinates.shape, BF), order_like],
        flops=1 << 28,
    )
    inner = lax.ppermute(inner, "leaf", [(i, i ^ 1) for i in range(count)])
    pairs = [(i, i + 1) for i in range(1, count - 1, 2)]
    across = lax.ppermute(across, "leaf", pairs + [(j, i) for i, j in pairs])
    late_low, late_high = call(
        weights_kernel,
        [low_like, high_like],
        [(VMEM, top_transfer), (VMEM, top_coupling)],
        flops=1 << 30,
    )
    message, field = call(
        middle_kernel,
        [((2 * NHIGH, 8, 2 * RANK), F32), ((COLS, RANK), F32)],
        [(VMEM, received), (VMEM, early_low), (VMEM, late_low)],
        scratch=[((2 * COLS, 6 * RANK), F32)],
        flops=1 << 27,
    )
    received = lax.all_to_all(message, "leaf", 0, 0, axis_index_groups=high_groups, tiled=True)
    coupling = far_coupling.transpose(1, 2, 0)
    (partial,) = call(
        local_kernel,
        [((COLS, PTS), F32)],
        [
            (SMEM, near_pairs),
            (SMEM, far_pairs),
            (ANY, field),
            (VMEM, coupling),
            (VMEM, leaf_basis),
            (VMEM, sorted_rhs),
            (VMEM, points),
            (VMEM, inner),
            (VMEM, across),
        ],
        scratch=[
            ((LEAF, RANK // 2, 2 * RANK), F32),
            ((LEAVES, 4 * COLS, 2 * RANK), BF),
            ((LEAVES, RANK // 2, 4 * COLS), F32),
            ((LEAVES + 2, COLS, LEAF), BF),
            ((LEAVES + 2, LEAF, COLS), BF),
            ((LEAVES + 2, COLS, LEAF), BF),
            ((LEAVES, COLS, LEAF), F32),
        ],
        flops=1 << 32,
        transcendentals=1 << 21,
    )
    (product,) = call(
        down_kernel,
        [((COLS, PTS), F32)],
        [
            (VMEM, received),
            (VMEM, early_high),
            (VMEM, late_high),
            (VMEM, field),
            (VMEM, partial),
            (HBM, leaf_transfer),
            (HBM, leaf_basis),
            (HBM, order),
        ],
        buffers=[transfer_like, basis_like, order_like],
        flops=1 << 28,
    )
    return product


def solution(mesh):
    return jax.shard_map(
        per_device,
        mesh=mesh,
        in_specs=(
            P(None, "leaf"),
            P(None, "leaf"),
            P("leaf"),
            P("leaf", None, None),
            P(None, "leaf"),
            P("leaf", None, None),
            P(None, "leaf"),
            P("leaf", None, None),
            P(),
            P(),
        ),
        out_specs=P(None, "leaf"),
        check_vma=False,
    )
```
